32 devices in a mesh: groups: 2 (over y), dp: 4 (over z), expert: 4 (over x, core).
Axes of the slice: x: 2, y: 2, z: 4, core: 2. Of those that a mesh axis runs over, the one named last changes fastest.
Arguments:
- output_gradient: bfloat16 [1024, 3072], P(('groups', 'dp'), 'expert'), parts along dimension 0, may hold values from -6 to 6
- hidden: bfloat16 [4, 1024, 8192], P('expert', 'groups', 'dp'), parts along dimension 1, may hold values from -0.59765625 to 0.59765625
- down_matrix: bfloat16 [4, 8192, 3072], P('expert', 'dp'), may hold values from -0.0625 to 0.0625
- adapter_down_matrix: bfloat16 [4, 8192, 512], P('expert', 'dp'), may hold values from -0.0625 to 0.0625
- adapter_up_matrix: bfloat16 [4, 512, 3072], P('expert', None, 'dp'), may hold values from -0.109375 to 0.109375
- routes: int32 [1024, 2], P(('groups', 'dp')), parts along dimension 0, may hold values from 0 to 3, all different within a row; in each aligned block of 128 rows (0 to 127, 128 to 255, ...) at most 128 rows name the same one
- router_weight: bfloat16 [1024, 2], P(('groups', 'dp')), parts along dimension 0, may hold values from 0.099609375 to 0.8984375
- tenant: int32 [1024], P(('groups', 'dp')), parts along dimension 0, may hold values from 0 to 15
Outputs:
- hidden_gradient: bfloat16 [4, 1024, 8192], P('expert', 'groups', 'dp'), parts along dimension 1
- adapter_down_gradient: float32 [8, 8192, 512], P(('groups', 'expert'), 'dp'), parts along dimension 0
- adapter_up_gradient: float32 [8, 512, 3072], P(('groups', 'expert'), None, 'dp'), parts along dimension 0
- router_gradient: float32 [1024, 2], P(('groups', 'dp')), parts along dimension 0
The draws below stay inside these ranges and needn't reach their ends.
There are 2 independent parts, one for each index of `groups`. The reference program is written for one: setup_inputs(seed, part) draws one part's arguments, and reference() takes and returns one part's arrays. A program takes and returns all parts, laid end to end along the dimension named above; an argument that names none is the same for every part. Nothing has to cross between parts.
Inputs may be any that keep to these rules, and one draw needn't show every extreme that they name: `routes`: within the 128 tokens of one index of dp no expert is named more than 128 times, and in some such block an expert is named exactly 128 times; the two experts of a token differ.
All inputs are finite; a program needn't handle non-finite values.
Results may differ from the reference program's by a relative error of at most 0.0029.
Values may be sent and summed in bfloat16 or wider, within the bound.
A program may use at most 128 MiB of HBM per device.

```python
import math
import jax
import jax.numpy as jnp
import numpy as np
from jax import lax

MODEL_WIDTH = 3072
HIDDEN_UNITS = 8192
ADAPTER_RANK = 32
TENANT_COUNT = 16
TOK = 128
EXPERT_COUNT = 4
CAP = 128
SLOTS = 512
NTOK = 512
N_DP = 4


def touch_ends(array, own_key, smallest, high):
    dims = array.shape
    spot = [jax.random.randint(jax.random.fold_in(own_key, axis), (), 0, dims[axis]) for axis in range(len(dims))]
    array = array.at[tuple(spot)].set(smallest)
    longest = dims.index(max(dims))
    spot[longest] = (spot[longest] + 1) % dims[longest]
    return array.at[tuple(spot)].set(high)


def steps_of(stream_key, shape, cuts, low, top_value):
    level = 1.0
    for position, parts in cuts:
        heights = jax.random.uniform(jax.random.fold_in(jax.random.fold_in(stream_key, 6), position), (parts,), jnp.float32, low / len(cuts), top_value / len(cuts))
        level = level * jnp.repeat(jnp.exp(heights), shape[position] // parts).reshape((-1,) + (1,) * (len(shape) - 1 - position))
    return level


def routed_block(rng, own, number, rows, number_of, top, bound, lean):
    sequence = jax.random.permutation(rng, number_of)
    crowded, ordinary = portions_of(number_of, rows * top, bound, lean, True), portions_of(number_of, rows * top, bound, lean, False)
    places = jnp.arange(number_of)

    def named(lengths, turn):
        used = int((lengths > 0).sum())
        fixed = max(1, used // 4)
        passed = fixed + (places - fixed + turn * (used - fixed)) % max(1, number_of - fixed)
        return jnp.zeros((number_of,), jnp.int32).at[sequence[jnp.where(places < fixed, places, passed)]].set(jnp.asarray(lengths, jnp.int32))

    lengths = jnp.where(number % 4 == 0, named(crowded, number // 4), named(ordinary, number - number // 4 - 1))
    mixed = jax.random.permutation(jax.random.fold_in(own, 3), number_of)
    donor, taker = mixed[0:number_of // 2 * 2:2], mixed[1:number_of // 2 * 2:2]
    room = jnp.minimum(lengths[donor] - 1, bound - lengths[taker]) // 2
    room = jnp.where((donor == sequence[0]) | (taker == sequence[0]) | (lengths[taker] == 0), 0, jnp.maximum(room, 0))
    passed = jax.random.randint(jax.random.fold_in(own, 4), (number_of // 2,), 0, 1 << 20) % (room + 1)
    lengths = lengths.at[donor].add(-passed).at[taker].add(passed)
    labels = jnp.searchsorted(jnp.cumsum(lengths), jnp.arange(rows * top), side="right").astype(jnp.int32)
    grid = labels.reshape(top, rows).T
    grid = grid[jax.random.permutation(jax.random.fold_in(own, 1), rows)]
    turn = jax.random.randint(jax.random.fold_in(own, 2), (rows, 1), 0, top)
    return jnp.take_along_axis(grid, (jnp.arange(top)[None, :] + turn) % top, axis=1)


def portions_of(number_of, total, reach, slope, full):
    loads = [(1 << 20) // math.isqrt(rank ** slope) + 1 for rank in range(1, number_of + 1)]
    largest = reach if full else min(reach, max(-(-total // number_of), total * loads[0] // sum(loads)))
    least = 1 if total - largest >= number_of - 1 else 0
    given, surplus = [largest] + [least] * (number_of - 1), total - largest - least * (number_of - 1)
    while surplus > 0:
        free = [i for i in range(1, number_of) if given[i] < largest] or [i for i in range(1, number_of) if given[i] < reach]
        pool, left = sum([loads[i] for i in free]), surplus
        for i in free:
            more = min(reach - given[i], max(1, left * loads[i] // pool), surplus)
            given[i] = given[i] + more
            surplus = surplus - more
    return np.array(given)


def gaussian(stream_key, extent, width, limit, pieces=(), kind=jnp.bfloat16):
    result = jax.random.normal(stream_key, extent, jnp.float32) * width
    if len(pieces) > 0:
        result = steps_of(stream_key, extent, pieces, -0.22, 0.18) * result
    return jnp.clip(result, min=-limit, max=limit).astype(kind)


def setup_inputs(seed: int = 0, part: int = 0) -> dict:
    seeds = jax.random.split(jax.random.key(seed), 9)
    own_keys = jax.random.split(jax.random.fold_in(seeds[8], part), 9)
    output_gradient = gaussian(own_keys[0], (NTOK, MODEL_WIDTH), 1.0, 6.0, ((0, 4), (1, 4)))
    hidden = gaussian(own_keys[1], (EXPERT_COUNT, SLOTS, HIDDEN_UNITS), 0.1, 0.59765625, ((0, 4), (2, 4)))
    down_matrix = gaussian(seeds[2], (EXPERT_COUNT, HIDDEN_UNITS, MODEL_WIDTH), HIDDEN_UNITS ** -0.5, 0.0625, ((0, 4), (1, 4)))
    adapter_down_matrix = gaussian(seeds[3], (EXPERT_COUNT, HIDDEN_UNITS, TENANT_COUNT * ADAPTER_RANK), HIDDEN_UNITS ** -0.5, 0.0625, ((0, 4), (1, 4)))
    adapter_up_matrix = gaussian(seeds[4], (EXPERT_COUNT, TENANT_COUNT * ADAPTER_RANK, MODEL_WIDTH), MODEL_WIDTH ** -0.5, 0.109375, ((0, 4), (2, 4)))
    routes_keys = jax.random.split(jax.random.fold_in(own_keys[5], 1), NTOK // TOK)
    routes_turns = jax.random.permutation(jax.random.fold_in(own_keys[5], 3), NTOK // TOK)
    routes = jax.vmap(lambda own, number: routed_block(jax.random.fold_in(own_keys[5], 2), own, number, TOK, EXPERT_COUNT, 2, CAP, 2))(routes_keys, routes_turns).reshape((NTOK, 2))
    router_weight = jnp.clip(0.099609375 + 0.7988281 * jax.random.uniform(own_keys[6], (NTOK, 2), jnp.float32) ** steps_of(own_keys[6], (NTOK, 2), ((0, 4),), -0.2, 0.2), 0.099609375, 0.8984375).astype(jnp.bfloat16)
    tenant = touch_ends(jax.random.randint(own_keys[7], (NTOK,), 0, TENANT_COUNT), jax.random.fold_in(own_keys[7], 1), 0, TENANT_COUNT - 1).astype(jnp.int32)
    return {"output_gradient": output_gradient, "hidden": hidden, "down_matrix": down_matrix, "adapter_down_matrix": adapter_down_matrix, "adapter_up_matrix": adapter_up_matrix, "routes": routes, "router_weight": router_weight, "tenant": tenant}


adapter_scale = 2.0


def slot_numbers(routes):
    flattened = routes.reshape(N_DP, TOK * 2)
    expert_hits = (flattened[:, :, None] == jnp.arange(EXPERT_COUNT, dtype=jnp.int32)[None, None, :]).astype(jnp.int32)
    earlier = jnp.cumsum(expert_hits, axis=1) - expert_hits
    offset = jnp.sum(earlier * expert_hits, axis=2)
    source = jnp.arange(N_DP, dtype=jnp.int32)[:, None]
    return (source * CAP + offset).reshape(-1).astype(jnp.int32)


def tenant_mask(owner):
    return (owner[:, None] == jnp.arange(TENANT_COUNT, dtype=jnp.int32)[None, :]).astype(jnp.float32)


def select_rank_columns(matrix, owning_tenants):
    return jnp.sum(matrix.reshape(-1, TENANT_COUNT, ADAPTER_RANK) * owning_tenants[:, :, None], axis=1)


def expand_rank(values, owning_tenants):
    return (owning_tenants[:, :, None] * values[:, None, :]).reshape(-1, TENANT_COUNT * ADAPTER_RANK)


def reference(output_gradient, hidden, down_matrix, adapter_down_matrix, adapter_up_matrix, routes, router_weight, tenant):
    slot_index = slot_numbers(routes)
    expert_index = routes.reshape(-1).astype(jnp.int32)
    token_index = jnp.repeat(jnp.arange(NTOK, dtype=jnp.int32), 2)
    dispatched = jnp.zeros((EXPERT_COUNT, SLOTS, MODEL_WIDTH), jnp.bfloat16).at[expert_index, slot_index].set(output_gradient[token_index])
    weight_slot = jnp.zeros((EXPERT_COUNT, SLOTS), jnp.float32).at[expert_index, slot_index].set(router_weight.reshape(-1).astype(jnp.float32))
    owner_slot = jnp.zeros((EXPERT_COUNT, SLOTS), jnp.int32).at[expert_index, slot_index].set(jnp.repeat(tenant, 2))

    def single_expert(tenant_number):
        incoming_rows = dispatched[tenant_number]
        hidden_activation_rows = hidden[tenant_number]
        owning_tenants = tenant_mask(owner_slot[tenant_number])
        scale_factor = weight_slot[tenant_number][:, None]
        frozen_gradient = jnp.dot(incoming_rows, down_matrix[tenant_number].T, preferred_element_type=jnp.float32)
        inner_left_factor = select_rank_columns(jnp.dot(hidden_activation_rows, adapter_down_matrix[tenant_number], preferred_element_type=jnp.float32), owning_tenants)
        inner_right_factor = select_rank_columns(jnp.dot(incoming_rows, adapter_up_matrix[tenant_number].T, preferred_element_type=jnp.float32), owning_tenants)
        spread_right_factor = expand_rank(inner_right_factor, owning_tenants).astype(jnp.bfloat16)
        scaled_right_factor = (scale_factor * expand_rank(inner_right_factor, owning_tenants)).astype(jnp.bfloat16)
        scaled_left_factor = (scale_factor * expand_rank(inner_left_factor, owning_tenants)).astype(jnp.bfloat16)
        adapter_contribution = jnp.dot(spread_right_factor, adapter_down_matrix[tenant_number].T, preferred_element_type=jnp.float32)
        hidden_gradient = (scale_factor * (frozen_gradient + adapter_scale * adapter_contribution)).astype(jnp.bfloat16)
        first_route_gradient = adapter_scale * jnp.dot(hidden_activation_rows.T, scaled_right_factor, preferred_element_type=jnp.float32)
        second_route_gradient = adapter_scale * jnp.dot(scaled_left_factor.T, incoming_rows, preferred_element_type=jnp.float32)
        slot_weight_score = jnp.sum(hidden_activation_rows.astype(jnp.float32) * frozen_gradient, axis=1) + adapter_scale * jnp.sum(inner_left_factor * inner_right_factor, axis=1)
        return hidden_gradient, first_route_gradient, second_route_gradient, slot_weight_score

    hidden_gradient, adapter_down_gradient, adapter_up_gradient, slot_weight_score = lax.map(single_expert, jnp.arange(EXPERT_COUNT, dtype=jnp.int32))
    router_gradient = slot_weight_score[expert_index, slot_index].reshape(NTOK, 2)
    return hidden_gradient, adapter_down_gradient, adapter_up_gradient, router_gradient
```

```python
import functools

import jax
import jax.numpy as jnp
from jax import lax
from jax.experimental import pallas as pl
from jax.experimental.pallas import tpu as pltpu
from jax.sharding import PartitionSpec as P

ADAPTER_RANK = 32
TENANT_COUNT = 16


adapter_scale = 2.0


def slot_places(routes, experts, capacity):
    sources = routes.shape[0]
    flattened = routes.reshape(sources, -1)
    expert_hits = (
        flattened[:, :, None] == jnp.arange(experts, dtype=jnp.int32)[None, None, :]
    ).astype(jnp.int32)
    earlier = jnp.cumsum(expert_hits, axis=1) - expert_hits
    offset = jnp.sum(earlier * expert_hits, axis=2)
    target = flattened * capacity + offset
    return target[:, None, :] == jnp.arange(experts * capacity, dtype=jnp.int32)[None, :, None]


def tenant_mask(owner):
    return (owner[:, None] == jnp.arange(TENANT_COUNT, dtype=jnp.int32)[None, :]).astype(
        jnp.float32
    )


def select_rank_columns(matrix, owning_tenants):
    return jnp.sum(
        matrix.reshape(owning_tenants.shape[0], TENANT_COUNT, ADAPTER_RANK)
        * owning_tenants[:, :, None],
        axis=1,
    )


def expand_rank(values, owning_tenants):
    return (owning_tenants[:, :, None] * values[:, None, :]).reshape(
        owning_tenants.shape[0], TENANT_COUNT * ADAPTER_RANK
    )


def contract_matrices(left, right, left_dim, right_dim):
    return lax.dot_general(
        left, right, (((left_dim,), (right_dim,)), ((), ())), preferred_element_type=jnp.float32
    )


def rows_terms(
    dispatched,
    weight_slot,
    owner_slot,
    hidden_activation_rows,
    down_rows,
    adapter_input,
    adapter_output,
    shard_index,
):
    owning_tenants = tenant_mask(owner_slot)
    block_width = adapter_output.shape[1]
    feature_tile = lax.dynamic_slice_in_dim(dispatched, shard_index * block_width, block_width, 1)
    frozen_gradient = contract_matrices(dispatched, down_rows, 1, 1)
    inner_left_factor = select_rank_columns(
        jnp.dot(hidden_activation_rows, adapter_input, preferred_element_type=jnp.float32),
        owning_tenants,
    )
    inner_right_factor = select_rank_columns(
        contract_matrices(feature_tile, adapter_output, 1, 1), owning_tenants
    )
    partial_score = jnp.sum(hidden_activation_rows.astype(jnp.float32) * frozen_gradient, axis=1)
    return (
        frozen_gradient,
        inner_left_factor,
        inner_right_factor,
        partial_score,
        weight_slot.astype(jnp.float32),
        owner_slot,
        feature_tile,
    )


def body(
    output_gradient,
    hidden,
    down_matrix,
    adapter_down_matrix,
    adapter_up_matrix,
    routes,
    router_weight,
    tenant,
):
    experts = lax.axis_size("expert")
    expert_index = lax.axis_index("expert")
    shard_index = lax.axis_index("dp")
    token_count = output_gradient.shape[0]
    capacity = 4 * token_count // experts
    hidden_activation_rows = hidden[0]
    down_rows = down_matrix[0]
    adapter_input = adapter_down_matrix[0]
    adapter_output = adapter_up_matrix[0]
    own_table = slot_places(routes[None], experts, capacity)[0]
    token_match = (
        own_table.reshape(experts * capacity, token_count, 2).astype(jnp.bfloat16).sum(axis=2)
    )
    outgoing = jnp.dot(token_match, output_gradient, preferred_element_type=jnp.float32).astype(
        jnp.bfloat16
    )
    outgoing = outgoing.reshape(experts, capacity, -1)
    arrived = lax.all_to_all(outgoing, "expert", split_axis=0, concat_axis=2, tiled=True)[0]
    chosen = lax.dynamic_slice_in_dim(own_table, expert_index * capacity, capacity, 0)
    weight_slot = jnp.sum(
        jnp.where(chosen, router_weight.reshape(1, -1).astype(jnp.float32), 0.0), axis=1
    ).astype(jnp.bfloat16)
    owner_slot = jnp.sum(jnp.where(chosen, jnp.repeat(tenant, 2)[None, :], 0), axis=1)
    portion = lax.all_gather((arrived, weight_slot, owner_slot), "dp", axis=0, tiled=True)
    results = rows_terms(
        portion[0],
        portion[1],
        portion[2],
        hidden_activation_rows,
        down_rows,
        adapter_input,
        adapter_output,
        shard_index,
    )
    (
        frozen_gradient,
        inner_left_factor,
        inner_right_factor,
        partial_score,
        weight_float,
        owner_all,
        feature_tile,
    ) = results
    inner_left_factor, inner_right_factor = lax.psum((inner_left_factor, inner_right_factor), "dp")
    owned_score = lax.psum_scatter(partial_score, "dp", scatter_dimension=0, tiled=True)
    owned_left_factor = lax.dynamic_slice_in_dim(
        inner_left_factor, shard_index * capacity, capacity, 0
    )
    owned_right_factor = lax.dynamic_slice_in_dim(
        inner_right_factor, shard_index * capacity, capacity, 0
    )
    owned_score = owned_score + adapter_scale * jnp.sum(
        owned_left_factor * owned_right_factor, axis=1
    )
    returned = lax.all_gather(owned_score, "expert", axis=0, tiled=True)
    router_gradient = jnp.sum(jnp.where(own_table, returned[:, None], 0.0), axis=0).reshape(
        token_count, 2
    )
    owning_tenants = tenant_mask(owner_all)
    scale_factor = weight_float[:, None]
    spread_right_factor = expand_rank(inner_right_factor, owning_tenants)
    scaled_right_factor = (scale_factor * spread_right_factor).astype(jnp.bfloat16)
    scaled_left_factor = (scale_factor * expand_rank(inner_left_factor, owning_tenants)).astype(
        jnp.bfloat16
    )
    adapter_contribution = contract_matrices(
        spread_right_factor.astype(jnp.bfloat16), adapter_input, 1, 1
    )
    hidden_gradient = (
        scale_factor * (frozen_gradient + adapter_scale * adapter_contribution)
    ).astype(jnp.bfloat16)
    first_route_gradient = adapter_scale * contract_matrices(
        hidden_activation_rows, scaled_right_factor, 0, 0
    )
    second_route_gradient = adapter_scale * contract_matrices(
        scaled_left_factor, feature_tile, 0, 0
    )
    return (
        hidden_gradient[None],
        first_route_gradient[None],
        second_route_gradient[None],
        router_gradient,
    )


MESH = pl.DeviceIdType.MESH
LANES = 128


def dot_nt(left, right):
    return contract_matrices(left, right, 1, 1)


def fold_lanes(values, owners):
    lane_group = lax.broadcasted_iota(jnp.int32, owners.shape, 1) // ADAPTER_RANK
    total = jnp.zeros(owners.shape, jnp.float32)
    for part in range(TENANT_COUNT * ADAPTER_RANK // LANES):
        mine = owners == (lane_group + part * (LANES // ADAPTER_RANK)).astype(jnp.float32)
        total = total + jnp.where(mine, values[:, part * LANES : (part + 1) * LANES], 0.0)
    return repeat_groups(total)


def repeat_groups(values):
    values = values + pltpu.roll(values, 2 * ADAPTER_RANK, 1)
    return values + pltpu.roll(values, ADAPTER_RANK, 1)


def pack_rows(values):
    rows = values.shape[0] // 4
    lane_group = lax.broadcasted_iota(jnp.int32, (rows, LANES), 1) // ADAPTER_RANK
    total = values[:rows]
    for part in range(1, 4):
        total = jnp.where(lane_group == part, values[part * rows : (part + 1) * rows], total)
    return total


def unpack_rows(values):
    lane_group = lax.broadcasted_iota(jnp.int32, values.shape, 1) // ADAPTER_RANK
    return jnp.concatenate(
        [repeat_groups(jnp.where(lane_group == part, values, 0.0)) for part in range(4)], axis=0
    )


def spread_rows(values, owners):
    lane_group = lax.broadcasted_iota(jnp.int32, owners.shape, 1) // ADAPTER_RANK
    parts = []
    for part in range(TENANT_COUNT * ADAPTER_RANK // LANES):
        mine = owners == (lane_group + part * (LANES // ADAPTER_RANK)).astype(jnp.float32)
        parts.append(jnp.where(mine, values, 0.0))
    return jnp.concatenate(parts, axis=1)


def kernel(
    tiles,
    grad_ref,
    hidden_ref,
    down_ref,
    adown_ref,
    aup_ref,
    routes_ref,
    weight_ref,
    tenant_ref,
    hgrad_out,
    dgrad_out,
    ugrad_out,
    router_out,
    tok,
    disp,
    down_v,
    hid,
    hid_t,
    ain,
    aup,
    base,
    hg_v,
    dg_v,
    ug_v,
    u_acc,
    meta,
    place,
    w_row,
    own_row,
    u_buf,
    v_buf,
    u_sum,
    v_sum,
    sp_v,
    sc_v,
    sc_ut,
    score_acc,
    score_out,
    score_in,
    final_out,
    final_in,
    tok_recv,
    send_z,
    send_x,
    send_c,
    meta_send,
    meta_recv,
    u_send,
    u_recv,
    v_send,
    v_recv,
    score_send,
    score_recv,
    final_send,
    final_recv,
    load_sem,
    down_sem,
    hid_sem,
    out_sem,
    out_sem_hg,
    out_sem_dg,
):
    me = lax.axis_index("dp")
    expert = lax.axis_index("expert")
    across = lax.rem(expert + 2, 4)
    core = expert + 1 - 2 * lax.rem(expert, 2)
    diagonal = lax.rem(core + 2, 4)
    near = me // 2
    far = 1 - near
    width = hid.shape[2]
    f32 = jnp.float32
    bf16 = jnp.bfloat16

    own_copy = pltpu.make_async_copy(grad_ref, tok.at[expert, me], load_sem.at[0])
    ain_copy = pltpu.make_async_copy(adown_ref.at[0], ain, load_sem.at[1])
    aup_copy = pltpu.make_async_copy(aup_ref.at[0], aup, load_sem.at[2])
    hid_copies = [
        pltpu.make_async_copy(
            hidden_ref.at[0, :, pl.ds(j * width, width)], hid.at[j], hid_sem.at[j]
        )
        for j in range(tiles)
    ]
    down_copies = [
        pltpu.make_async_copy(
            down_ref.at[0, pl.ds(j * width, width), :], down_v.at[j], down_sem.at[j]
        )
        for j in range(tiles)
    ]
    own_copy.start()
    for copy in hid_copies:
        copy.start()
    ain_copy.start()
    aup_copy.start()
    for copy in down_copies:
        copy.start()
    meta[me, 0:2, :] = routes_ref[...].astype(f32)
    meta[me, 2:4, :] = weight_ref[...].astype(f32)
    meta[me, 4:5, :] = tenant_ref[...].astype(f32)
    meta[me, 5:8, :] = jnp.zeros((3, LANES), f32)

    barrier = pltpu.get_barrier_semaphore()
    for step in range(1, 4):
        pl.semaphore_signal(
            barrier, inc=1, device_id={"dp": lax.rem(me + step, 4)}, device_id_type=MESH
        )
        pl.semaphore_signal(
            barrier, inc=1, device_id={"expert": lax.rem(expert + step, 4)}, device_id_type=MESH
        )
    pl.semaphore_wait(barrier, 6)

    def remote(src, dst, send, recv, **target):
        return pltpu.make_async_remote_copy(
            src_ref=src,
            dst_ref=dst,
            send_sem=send,
            recv_sem=recv,
            device_id=target,
            device_id_type=MESH,
        )

    def to_left(p, src=None):
        block = tok.at[expert, p]
        return remote(
            block if src is None else src,
            block,
            send_z.at[0, p],
            tok_recv.at[expert, p],
            dp=jnp.maximum(me - 1, 0),
        )

    def to_right(p, src=None):
        block = tok.at[expert, p]
        return remote(
            block if src is None else src,
            block,
            send_z.at[1, p],
            tok_recv.at[expert, p],
            dp=jnp.minimum(me + 1, 3),
        )

    def to_across(p, src=None):
        block = tok.at[expert, p]
        return remote(
            block if src is None else src,
            block,
            send_x.at[p],
            tok_recv.at[expert, p],
            expert=across,
        )

    def to_core(q, slot, p, src=None):
        block = tok.at[q, p]
        return remote(
            block if src is None else src,
            block,
            send_c.at[slot, p],
            tok_recv.at[q, p],
            expert=core,
        )

    def arrived(q, p):
        block = tok.at[q, p]
        remote(block, block, send_c.at[0, p], tok_recv.at[q, p], expert=core).wait_recv()

    meta_copies = []
    for step in range(1, 4):
        copy = remote(
            meta.at[me],
            meta.at[me],
            meta_send.at[step - 1],
            meta_recv.at[me],
            dp=lax.rem(me + step, 4),
        )
        copy.start()
        meta_copies.append(copy)

    @pl.when(me > 0)
    def _():
        to_left(me, grad_ref).start()

    @pl.when(me < 3)
    def _():
        to_right(me, grad_ref).start()

    to_across(me, grad_ref).start()
    to_core(expert, 0, me, grad_ref).start()

    for step in range(1, 4):
        p = lax.rem(me + step, 4)
        remote(
            meta.at[p], meta.at[p], meta_send.at[0], meta_recv.at[p], dp=p
        ).wait_recv()
    expert_f = expert.astype(f32)
    row_ids = lax.broadcasted_iota(jnp.int32, (LANES, LANES), 0)
    col_ids = lax.broadcasted_iota(jnp.int32, (LANES, LANES), 1)
    before = (row_ids < col_ids).astype(bf16)
    for p in range(4):
        info = meta[p]
        first = info[0:1] == expert_f
        second = info[1:2] == expert_f
        hit = jnp.where(first | second, 1.0, 0.0)
        offset = jnp.dot(
            jnp.broadcast_to(hit, (16, LANES)).astype(bf16), before, preferred_element_type=f32
        )[0:1]
        offset = jnp.where(hit > 0.0, offset, -1.0)
        table = offset == row_ids.astype(f32)
        place[p] = jnp.where(table, 1.0, 0.0).astype(bf16)
        chosen = jnp.where(first, info[2:3], info[3:4])
        rows = pl.ds(p * LANES, LANES)
        w_row[rows] = jnp.broadcast_to(
            jnp.sum(jnp.where(table, chosen, 0.0), axis=1, keepdims=True), (LANES, LANES)
        )
        own_row[rows] = jnp.broadcast_to(
            jnp.sum(jnp.where(table, info[4:5], 0.0), axis=1, keepdims=True), (LANES, LANES)
        )

    for copy in hid_copies:
        copy.wait()
    ain_copy.wait()

    def add_u(j, carry):
        part = jnp.dot(
            hid[j], ain[pl.ds(pl.multiple_of(j * width, width), width), :], preferred_element_type=f32
        )
        u_acc[...] = jnp.where(j == 0, part, u_acc[...] + part)
        return carry

    u_acc[...] = jnp.zeros(u_acc.shape, f32)
    lax.fori_loop(0, tiles, add_u, 0)
    for pair in range(2):
        rows = slice(pair * 256, (pair + 1) * 256)
        u_buf[me, pair] = pack_rows(fold_lanes(u_acc[rows], own_row[rows]))
    u_copies = []
    for step in range(1, 4):
        copy = remote(
            u_buf.at[me],
            u_buf.at[me],
            u_send.at[step - 1],
            u_recv.at[me],
            dp=lax.rem(me + step, 4),
        )
        copy.start()
        u_copies.append(copy)

    def forward_z(distance):
        @pl.when(me >= distance)
        def _():
            p = jnp.maximum(me - distance, 0)
            arrived(expert, p)

            @pl.when(me < 3)
            def _():
                to_right(p).start()

            to_across(p).start()
            to_core(expert, 0, p).start()

        @pl.when(me + distance <= 3)
        def _():
            p = jnp.minimum(me + distance, 3)
            arrived(expert, p)

            @pl.when(me > 0)
            def _():
                to_left(p).start()

            to_across(p).start()
            to_core(expert, 0, p).start()

    def forward_x(distance):
        def one(p):
            arrived(across, p)
            to_core(across, 1, p).start()

        if distance == 0:
            one(me)
            return

        @pl.when(me >= distance)
        def _():
            one(jnp.maximum(me - distance, 0))

        @pl.when(me + distance <= 3)
        def _():
            one(jnp.minimum(me + distance, 3))

    def transpose_tiles(j, carry):
        hid_t[j] = hid[j].T
        return carry

    forward_z(1)
    forward_x(0)
    lax.fori_loop(0, tiles, transpose_tiles, 0)
    forward_z(2)
    forward_x(1)

    def dispatch(pair):
        for i in range(2):
            p = pair * 2 + i
            arrived(core, p)
            arrived(diagonal, p)
            for q in range(4):
                disp[q, pair, i * LANES : (i + 1) * LANES, :] = jnp.dot(
                    place[p], tok[q, p], preferred_element_type=f32
                ).astype(bf16)

    def send_v(pair, slot):
        rows = pl.ds(pl.multiple_of(pair * 256, 256), 256)
        values = dot_nt(disp[me, pair], aup[...])
        v_buf[me, pair] = pack_rows(fold_lanes(values, own_row[rows]))
        copies = []
        for step in range(1, 4):
            copy = remote(
                v_buf.at[me, pair],
                v_buf.at[me, pair],
                v_send.at[slot, step - 1],
                v_recv.at[me, pair],
                dp=lax.rem(me + step, 4),
            )
            copy.start()
            copies.append(copy)
        return copies

    def base_tiles(pair, first, last):
        rows = pl.ds(pl.multiple_of(pair * 256, 256), 256)

        def tile(j, carry):
            total = dot_nt(disp[0, pair], down_v[j, :, 0:768])
            for q in range(1, 4):
                total = total + dot_nt(disp[q, pair], down_v[j, :, q * 768 : (q + 1) * 768])
            base[j, pair] = total
            product = hid[j, rows, :].astype(f32) * total
            for part in range(width // LANES):
                score_acc[rows] += product[:, part * LANES : (part + 1) * LANES]
            return carry

        lax.fori_loop(first, last, tile, 0)

    own_copy.wait()
    score_acc[...] = jnp.zeros(score_acc.shape, f32)
    dispatch(near)
    aup_copy.wait()
    v_copies = send_v(near, 0)
    for copy in down_copies:
        copy.wait()
    half = tiles // 2
    base_tiles(near, 0, half)
    forward_z(3)
    forward_x(2)
    base_tiles(near, half, tiles)

    for step in range(1, 4):
        p = lax.rem(me + step, 4)
        remote(u_buf.at[p], u_buf.at[p], u_send.at[0], u_recv.at[p], dp=p).wait_recv()
    for pair in range(2):
        rows = slice(pair * 256, (pair + 1) * 256)
        total = ((u_buf[0, pair] + u_buf[1, pair]) + u_buf[2, pair]) + u_buf[3, pair]
        total = unpack_rows(total)
        u_sum[rows] = total
        sc_ut[:, rows] = spread_rows(w_row[rows] * total, own_row[rows]).T.astype(bf16)

    forward_x(3)
    dispatch(far)
    v_copies += send_v(far, 1)
    base_tiles(far, 0, tiles)

    for p in range(4):
        rows = slice(p * LANES, (p + 1) * LANES)
        score = jnp.sum(score_acc[rows], axis=1, keepdims=True)
        score_out[p] = jnp.broadcast_to(
            jnp.sum(place[p].astype(f32) * score, axis=0, keepdims=True), (8, LANES)
        )
    score_copies = []
    for step in range(1, 4):
        p = lax.rem(me + step, 4)
        copy = remote(
            score_out.at[p],
            score_in.at[me],
            score_send.at[step - 1],
            score_recv.at[me],
            dp=p,
        )
        copy.start()
        score_copies.append(copy)
    score_in[me] = score_out[me]

    ug_v[...] = adapter_scale * jnp.dot(
        sc_ut[...], disp[me].reshape(512, 768), preferred_element_type=f32
    )
    ug_copy = pltpu.make_async_copy(ug_v, ugrad_out.at[0], out_sem.at[0])
    ug_copy.start()

    for step in range(1, 4):
        p = lax.rem(me + step, 4)
        for pair in range(2):
            remote(
                v_buf.at[p, pair],
                v_buf.at[p, pair],
                v_send.at[0, 0],
                v_recv.at[p, pair],
                dp=p,
            ).wait_recv()
    for pair in range(2):
        rows = slice(pair * 256, (pair + 1) * 256)
        total = ((v_buf[0, pair] + v_buf[1, pair]) + v_buf[2, pair]) + v_buf[3, pair]
        total = unpack_rows(total)
        v_sum[rows] = total
        sp_v[rows] = spread_rows(total, own_row[rows]).astype(bf16)
        sc_v[rows] = spread_rows(w_row[rows] * total, own_row[rows]).astype(bf16)

    for step in range(1, 4):
        p = lax.rem(me + step, 4)
        remote(score_in.at[p], score_in.at[p], score_send.at[0], score_recv.at[p], dp=p).wait_recv()
    rows = pl.ds(pl.multiple_of(me * LANES, LANES), LANES)
    inner = (adapter_scale / 4) * jnp.sum(u_sum[rows] * v_sum[rows], axis=1, keepdims=True)
    inner = jnp.sum(place[me].astype(f32) * inner, axis=0, keepdims=True)
    total = ((score_in[0] + score_in[1]) + score_in[2]) + score_in[3]
    final_out[...] = total + inner
    final_copies = []
    for step in range(1, 4):
        e = lax.rem(expert + step, 4)
        copy = remote(
            final_out,
            final_in.at[expert],
            final_send.at[step - 1],
            final_recv.at[expert],
            expert=e,
        )
        copy.start()
        final_copies.append(copy)
    final_in[expert] = final_out[...]

    def out_down(j):
        return pltpu.make_async_copy(
            dg_v.at[j], dgrad_out.at[0, pl.ds(j * width, width), :], out_sem_dg.at[j]
        )

    def out_hidden(j):
        return pltpu.make_async_copy(
            hg_v.at[j],
            hgrad_out.at[0, :, pl.ds(pl.multiple_of(j * width, width), width)],
            out_sem_hg.at[j],
        )

    def finish(j, carry):
        dg_v[j] = adapter_scale * jnp.dot(hid_t[j], sc_v[...], preferred_element_type=f32)
        out_down(j).start()
        extra = dot_nt(
            sp_v[...], ain[pl.ds(pl.multiple_of(j * width, width), width), :]
        )
        scale = w_row[...]
        scale = jnp.concatenate([scale] * (width // LANES), axis=1)
        hg_v[j] = (
            scale * (base[j].reshape(512, width) + adapter_scale * extra)
        ).astype(bf16)
        out_hidden(j).start()
        return carry

    lax.fori_loop(0, tiles, finish, 0)

    for step in range(1, 4):
        e = lax.rem(expert + step, 4)
        remote(
            final_in.at[e], final_in.at[e], final_send.at[0], final_recv.at[e], expert=e
        ).wait_recv()
    chosen = meta[me, 0:2, :]
    total = jnp.zeros((2, LANES), f32)
    for e in range(4):
        total = total + jnp.where(chosen == float(e), final_in[e, 0:1, :], 0.0)
    router_out[...] = total

    for copy in meta_copies + u_copies + v_copies + score_copies + final_copies:
        copy.wait_send()
    for p in range(4):
        to_across(p).wait_send()
        to_core(expert, 0, p).wait_send()
        to_core(across, 1, p).wait_send()

        @pl.when((me > 0) & (me <= p))
        def _():
            to_left(p).wait_send()

        @pl.when((me < 3) & (me >= p))
        def _():
            to_right(p).wait_send()

    ug_copy.wait()
    for j in range(tiles):
        out_down(j).wait()
        out_hidden(j).wait()


def kernel_body(
    output_gradient,
    hidden,
    down_matrix,
    adapter_down_matrix,
    adapter_up_matrix,
    routes,
    router_weight,
    tenant,
):
    width = 256
    tokens, features = output_gradient.shape
    _, slots, units = hidden.shape
    model = down_matrix.shape[2]
    spread = adapter_down_matrix.shape[2]
    tiles = units // width
    f32 = jnp.float32
    bf16 = jnp.bfloat16
    dma = pltpu.SemaphoreType.DMA
    vmem = pl.BlockSpec(memory_space=pltpu.VMEM)
    hbm = pl.BlockSpec(memory_space=pl.ANY)
    hgrad, dgrad, ugrad, router = pl.pallas_call(
        functools.partial(kernel, tiles),
        out_shape=(
            jax.ShapeDtypeStruct(hidden.shape, bf16),
            jax.ShapeDtypeStruct(adapter_down_matrix.shape, f32),
            jax.ShapeDtypeStruct(adapter_up_matrix.shape, f32),
            jax.ShapeDtypeStruct((2, tokens), f32),
        ),
        in_specs=[hbm] * 5 + [vmem] * 3,
        out_specs=(hbm, hbm, hbm, vmem),
        scratch_shapes=[
            pltpu.VMEM((4, 4, tokens, features), bf16),
            pltpu.VMEM((4, 2, 256, features), bf16),
            pltpu.VMEM((tiles, width, model), bf16),
            pltpu.VMEM((tiles, slots, width), bf16),
            pltpu.VMEM((tiles, width, slots), bf16),
            pltpu.VMEM((units, spread), bf16),
            pltpu.VMEM((spread, features), bf16),
            pltpu.VMEM((tiles, 2, 256, width), f32),
            pltpu.VMEM((tiles, slots, width), bf16),
            pltpu.VMEM((tiles, width, spread), f32),
            pltpu.VMEM((spread, features), f32),
            pltpu.VMEM((slots, spread), f32),
            pltpu.VMEM((4, 8, LANES), f32),
            pltpu.VMEM((4, LANES, LANES), bf16),
            pltpu.VMEM((slots, LANES), f32),
            pltpu.VMEM((slots, LANES), f32),
            pltpu.VMEM((4, 2, 64, LANES), f32),
            pltpu.VMEM((4, 2, 64, LANES), f32),
            pltpu.VMEM((slots, LANES), f32),
            pltpu.VMEM((slots, LANES), f32),
            pltpu.VMEM((slots, spread), bf16),
            pltpu.VMEM((slots, spread), bf16),
            pltpu.VMEM((spread, slots), bf16),
            pltpu.VMEM((slots, LANES), f32),
            pltpu.VMEM((4, 8, LANES), f32),
            pltpu.VMEM((4, 8, LANES), f32),
            pltpu.VMEM((8, LANES), f32),
            pltpu.VMEM((4, 8, LANES), f32),
            dma((4, 4)),
            dma((2, 4)),
            dma((4,)),
            dma((2, 4)),
            dma((3,)),
            dma((4,)),
            dma((3,)),
            dma((4,)),
            dma((2, 3)),
            dma((4, 2)),
            dma((3,)),
            dma((4,)),
            dma((3,)),
            dma((4,)),
            dma((3,)),
            dma((tiles,)),
            dma((tiles,)),
            dma((1,)),
            dma((tiles,)),
            dma((tiles,)),
        ],
        compiler_params=pltpu.CompilerParams(
            collective_id=0, has_side_effects=True, vmem_limit_bytes=58 * 1024 * 1024
        ),
    )(
        output_gradient,
        hidden,
        down_matrix,
        adapter_down_matrix,
        adapter_up_matrix,
        routes.T,
        router_weight.T,
        tenant[None, :],
    )
    return hgrad, dgrad, ugrad, router.T


def fitting_body(mesh, *arrays):
    gradient, hidden, down = arrays[0], arrays[1], arrays[2]
    fits = (
        mesh.shape["dp"] == 4
        and mesh.shape["expert"] == 4
        and gradient.shape == (128, 768)
        and hidden.shape[1] == 512
        and hidden.shape[2] % 512 == 0
        and hidden.shape[2] <= 2048
        and down.shape[2] == 3072
    )
    return (kernel_body if fits else body)(*arrays)


def solution(mesh):
    in_specs = (
        P(("groups", "dp"), "expert"),
        P("expert", "groups", "dp"),
        P("expert", "dp", None),
        P("expert", "dp", None),
        P("expert", None, "dp"),
        P(("groups", "dp"), None),
        P(("groups", "dp"), None),
        P(("groups", "dp")),
    )
    out_specs = (
        P("expert", "groups", "dp"),
        P(("groups", "expert"), "dp", None),
        P(("groups", "expert"), None, "dp"),
        P(("groups", "dp"), None),
    )
    return jax.shard_map(
        functools.partial(fitting_body, mesh),
        mesh=mesh,
        in_specs=in_specs,
        out_specs=out_specs,
        check_vma=False,
    )
```

```python
import functools

import jax
import jax.numpy as jnp
from jax import lax
from jax.experimental import pallas as pl
from jax.experimental.pallas import tpu as pltpu
from jax.sharding import PartitionSpec as P

ADAPTER_RANK = 32
TENANT_COUNT = 16


adapter_scale = 2.0


def slot_places(routes, experts, capacity):
    sources = routes.shape[0]
    flattened = routes.reshape(sources, -1)
    expert_hits = (
        flattened[:, :, None] == jnp.arange(experts, dtype=jnp.int32)[None, None, :]
    ).astype(jnp.int32)
    earlier = jnp.cumsum(expert_hits, axis=1) - expert_hits
    offset = jnp.sum(earlier * expert_hits, axis=2)
    target = flattened * capacity + offset
    return target[:, None, :] == jnp.arange(experts * capacity, dtype=jnp.int32)[None, :, None]


def tenant_mask(owner):
    return (owner[:, None] == jnp.arange(TENANT_COUNT, dtype=jnp.int32)[None, :]).astype(
        jnp.float32
    )


def select_rank_columns(matrix, owning_tenants):
    return jnp.sum(
        matrix.reshape(owning_tenants.shape[0], TENANT_COUNT, ADAPTER_RANK)
        * owning_tenants[:, :, None],
        axis=1,
    )


def expand_rank(values, owning_tenants):
    return (owning_tenants[:, :, None] * values[:, None, :]).reshape(
        owning_tenants.shape[0], TENANT_COUNT * ADAPTER_RANK
    )


def contract_matrices(left, right, left_dim, right_dim):
    return lax.dot_general(
        left, right, (((left_dim,), (right_dim,)), ((), ())), preferred_element_type=jnp.float32
    )


def rows_terms(
    dispatched,
    weight_slot,
    owner_slot,
    hidden_activation_rows,
    down_rows,
    adapter_input,
    adapter_output,
    shard_index,
):
    owning_tenants = tenant_mask(owner_slot)
    block_width = adapter_output.shape[1]
    feature_tile = lax.dynamic_slice_in_dim(dispatched, shard_index * block_width, block_width, 1)
    frozen_gradient = contract_matrices(dispatched, down_rows, 1, 1)
    inner_left_factor = select_rank_columns(
        jnp.dot(hidden_activation_rows, adapter_input, preferred_element_type=jnp.float32),
        owning_tenants,
    )
    inner_right_factor = select_rank_columns(
        contract_matrices(feature_tile, adapter_output, 1, 1), owning_tenants
    )
    partial_score = jnp.sum(hidden_activation_rows.astype(jnp.float32) * frozen_gradient, axis=1)
    return (
        frozen_gradient,
        inner_left_factor,
        inner_right_factor,
        partial_score,
        weight_slot.astype(jnp.float32),
        owner_slot,
        feature_tile,
    )


def body(
    output_gradient,
    hidden,
    down_matrix,
    adapter_down_matrix,
    adapter_up_matrix,
    routes,
    router_weight,
    tenant,
):
    experts = lax.axis_size("expert")
    expert_index = lax.axis_index("expert")
    shard_index = lax.axis_index("dp")
    token_count = output_gradient.shape[0]
    capacity = 4 * token_count // experts
    hidden_activation_rows = hidden[0]
    down_rows = down_matrix[0]
    adapter_input = adapter_down_matrix[0]
    adapter_output = adapter_up_matrix[0]
    own_table = slot_places(routes[None], experts, capacity)[0]
    token_match = (
        own_table.reshape(experts * capacity, token_count, 2).astype(jnp.bfloat16).sum(axis=2)
    )
    outgoing = jnp.dot(token_match, output_gradient, preferred_element_type=jnp.float32).astype(
        jnp.bfloat16
    )
    outgoing = outgoing.reshape(experts, capacity, -1)
    arrived = lax.all_to_all(outgoing, "expert", split_axis=0, concat_axis=2, tiled=True)[0]
    chosen = lax.dynamic_slice_in_dim(own_table, expert_index * capacity, capacity, 0)
    weight_slot = jnp.sum(
        jnp.where(chosen, router_weight.reshape(1, -1).astype(jnp.float32), 0.0), axis=1
    ).astype(jnp.bfloat16)
    owner_slot = jnp.sum(jnp.where(chosen, jnp.repeat(tenant, 2)[None, :], 0), axis=1)
    portion = lax.all_gather((arrived, weight_slot, owner_slot), "dp", axis=0, tiled=True)
    results = rows_terms(
        portion[0],
        portion[1],
        portion[2],
        hidden_activation_rows,
        down_rows,
        adapter_input,
        adapter_output,
        shard_index,
    )
    (
        frozen_gradient,
        inner_left_factor,
        inner_right_factor,
        partial_score,
        weight_float,
        owner_all,
        feature_tile,
    ) = results
    inner_left_factor, inner_right_factor = lax.psum((inner_left_factor, inner_right_factor), "dp")
    owned_score = lax.psum_scatter(partial_score, "dp", scatter_dimension=0, tiled=True)
    owned_left_factor = lax.dynamic_slice_in_dim(
        inner_left_factor, shard_index * capacity, capacity, 0
    )
    owned_right_factor = lax.dynamic_slice_in_dim(
        inner_right_factor, shard_index * capacity, capacity, 0
    )
    owned_score = owned_score + adapter_scale * jnp.sum(
        owned_left_factor * owned_right_factor, axis=1
    )
    returned = lax.all_gather(owned_score, "expert", axis=0, tiled=True)
    router_gradient = jnp.sum(jnp.where(own_table, returned[:, None], 0.0), axis=0).reshape(
        token_count, 2
    )
    owning_tenants = tenant_mask(owner_all)
    scale_factor = weight_float[:, None]
    spread_right_factor = expand_rank(inner_right_factor, owning_tenants)
    scaled_right_factor = (scale_factor * spread_right_factor).astype(jnp.bfloat16)
    scaled_left_factor = (scale_factor * expand_rank(inner_left_factor, owning_tenants)).astype(
        jnp.bfloat16
    )
    adapter_contribution = contract_matrices(
        spread_right_factor.astype(jnp.bfloat16), adapter_input, 1, 1
    )
    hidden_gradient = (
        scale_factor * (frozen_gradient + adapter_scale * adapter_contribution)
    ).astype(jnp.bfloat16)
    first_route_gradient = adapter_scale * contract_matrices(
        hidden_activation_rows, scaled_right_factor, 0, 0
    )
    second_route_gradient = adapter_scale * contract_matrices(
        scaled_left_factor, feature_tile, 0, 0
    )
    return (
        hidden_gradient[None],
        first_route_gradient[None],
        second_route_gradient[None],
        router_gradient,
    )


MESH = pl.DeviceIdType.MESH
LANES = 128


def dot_nt(left, right):
    return contract_matrices(left, right, 1, 1)


def fold_lanes(values, owners):
    lane_group = lax.broadcasted_iota(jnp.int32, owners.shape, 1) // ADAPTER_RANK
    total = jnp.zeros(owners.shape, jnp.float32)
    for part in range(TENANT_COUNT * ADAPTER_RANK // LANES):
        mine = owners == (lane_group + part * (LANES // ADAPTER_RANK)).astype(jnp.float32)
        total = total + jnp.where(mine, values[:, part * LANES : (part + 1) * LANES], 0.0)
    return repeat_groups(total)


def repeat_groups(values):
    values = values + pltpu.roll(values, 2 * ADAPTER_RANK, 1)
    return values + pltpu.roll(values, ADAPTER_RANK, 1)


def pack_rows(values):
    rows = values.shape[0] // 4
    lane_group = lax.broadcasted_iota(jnp.int32, (rows, LANES), 1) // ADAPTER_RANK
    total = values[:rows]
    for part in range(1, 4):
        total = jnp.where(lane_group == part, values[part * rows : (part + 1) * rows], total)
    return total


def unpack_rows(values):
    lane_group = lax.broadcasted_iota(jnp.int32, values.shape, 1) // ADAPTER_RANK
    return jnp.concatenate(
        [repeat_groups(jnp.where(lane_group == part, values, 0.0)) for part in range(4)], axis=0
    )


def spread_rows(values, owners):
    lane_group = lax.broadcasted_iota(jnp.int32, owners.shape, 1) // ADAPTER_RANK
    parts = []
    for part in range(TENANT_COUNT * ADAPTER_RANK // LANES):
        mine = owners == (lane_group + part * (LANES // ADAPTER_RANK)).astype(jnp.float32)
        parts.append(jnp.where(mine, values, 0.0))
    return jnp.concatenate(parts, axis=1)


def kernel(
    tiles,
    grad_ref,
    hidden_ref,
    down_ref,
    adown_ref,
    aup_ref,
    routes_ref,
    weight_ref,
    tenant_ref,
    hgrad_out,
    turned_out,
    sc_v_out,
    sc_ut_out,
    feat_out,
    router_out,
    tok,
    disp,
    down_v,
    hid,
    hid_t,
    ain,
    aup,
    base,
    hg_v,
    u_acc,
    meta,
    place,
    w_row,
    own_row,
    u_buf,
    v_buf,
    u_sum,
    v_sum,
    sp_v,
    sc_v,
    sc_ut,
    score_acc,
    score_out,
    score_in,
    tok_recv,
    send_z,
    send_x,
    send_c,
    meta_send,
    meta_recv,
    u_send,
    u_recv,
    v_send,
    v_recv,
    score_send,
    score_recv,
    load_sem,
    down_sem,
    hid_sem,
    out_sem,
    out_sem_hg,
):
    me = lax.axis_index("dp")
    expert = lax.axis_index("expert")
    across = lax.rem(expert + 2, 4)
    core = expert + 1 - 2 * lax.rem(expert, 2)
    diagonal = lax.rem(core + 2, 4)
    near = me // 2
    far = 1 - near
    width = hid.shape[2]
    f32 = jnp.float32
    bf16 = jnp.bfloat16

    own_copy = pltpu.make_async_copy(grad_ref, tok.at[expert, me], load_sem.at[0])
    ain_copy = pltpu.make_async_copy(adown_ref.at[0], ain, load_sem.at[1])
    aup_copy = pltpu.make_async_copy(aup_ref.at[0], aup, load_sem.at[2])
    hid_copies = [
        pltpu.make_async_copy(
            hidden_ref.at[0, :, pl.ds(j * width, width)], hid.at[j], hid_sem.at[j]
        )
        for j in range(tiles)
    ]
    down_copies = [
        pltpu.make_async_copy(
            down_ref.at[0, pl.ds(j * width, width), :], down_v.at[j], down_sem.at[j]
        )
        for j in range(tiles)
    ]
    own_copy.start()
    for copy in hid_copies:
        copy.start()
    ain_copy.start()
    aup_copy.start()
    for copy in down_copies:
        copy.start()
    meta[me, 0:2, :] = routes_ref[...].astype(f32)
    meta[me, 2:4, :] = weight_ref[...].astype(f32)
    meta[me, 4:5, :] = tenant_ref[...].astype(f32)
    meta[me, 5:8, :] = jnp.zeros((3, LANES), f32)

    barrier = pltpu.get_barrier_semaphore()
    for step in range(1, 16):
        pl.semaphore_signal(
            barrier,
            inc=1,
            device_id={
                "dp": lax.rem(me + step // 4, 4),
                "expert": lax.rem(expert + step % 4, 4),
            },
            device_id_type=MESH,
        )
    pl.semaphore_wait(barrier, 15)

    def remote(src, dst, send, recv, **target):
        return pltpu.make_async_remote_copy(
            src_ref=src,
            dst_ref=dst,
            send_sem=send,
            recv_sem=recv,
            device_id=target,
            device_id_type=MESH,
        )

    def to_left(p, src=None):
        block = tok.at[expert, p]
        return remote(
            block if src is None else src,
            block,
            send_z.at[0, p],
            tok_recv.at[expert, p],
            dp=jnp.maximum(me - 1, 0),
        )

    def to_right(p, src=None):
        block = tok.at[expert, p]
        return remote(
            block if src is None else src,
            block,
            send_z.at[1, p],
            tok_recv.at[expert, p],
            dp=jnp.minimum(me + 1, 3),
        )

    def to_across(p, src=None):
        block = tok.at[expert, p]
        return remote(
            block if src is None else src,
            block,
            send_x.at[p],
            tok_recv.at[expert, p],
            expert=across,
        )

    def to_core(q, slot, p, src=None):
        block = tok.at[q, p]
        return remote(
            block if src is None else src,
            block,
            send_c.at[slot, p],
            tok_recv.at[q, p],
            expert=core,
        )

    def arrived(q, p):
        block = tok.at[q, p]
        remote(block, block, send_c.at[0, p], tok_recv.at[q, p], expert=core).wait_recv()

    meta_copies = []
    for step in range(1, 4):
        copy = remote(
            meta.at[me],
            meta.at[me],
            meta_send.at[step - 1],
            meta_recv.at[me],
            dp=lax.rem(me + step, 4),
        )
        copy.start()
        meta_copies.append(copy)

    @pl.when(me > 0)
    def _():
        to_left(me, grad_ref).start()

    @pl.when(me < 3)
    def _():
        to_right(me, grad_ref).start()

    to_across(me, grad_ref).start()
    to_core(expert, 0, me, grad_ref).start()

    for step in range(1, 4):
        p = lax.rem(me + step, 4)
        remote(
            meta.at[p], meta.at[p], meta_send.at[0], meta_recv.at[p], dp=p
        ).wait_recv()
    expert_f = expert.astype(f32)
    row_ids = lax.broadcasted_iota(jnp.int32, (LANES, LANES), 0)
    col_ids = lax.broadcasted_iota(jnp.int32, (LANES, LANES), 1)
    before = (row_ids < col_ids).astype(bf16)
    for p in range(4):
        info = meta[p]
        first = info[0:1] == expert_f
        second = info[1:2] == expert_f
        hit = jnp.where(first | second, 1.0, 0.0)
        offset = jnp.dot(
            jnp.broadcast_to(hit, (16, LANES)).astype(bf16), before, preferred_element_type=f32
        )[0:1]
        offset = jnp.where(hit > 0.0, offset, -1.0)
        table = offset == row_ids.astype(f32)
        place[p] = jnp.where(table, 1.0, 0.0).astype(bf16)
        chosen = jnp.where(first, info[2:3], info[3:4])
        rows = pl.ds(p * LANES, LANES)
        w_row[rows] = jnp.broadcast_to(
            jnp.sum(jnp.where(table, chosen, 0.0), axis=1, keepdims=True), (LANES, LANES)
        )
        own_row[rows] = jnp.broadcast_to(
            jnp.sum(jnp.where(table, info[4:5], 0.0), axis=1, keepdims=True), (LANES, LANES)
        )

    for copy in hid_copies:
        copy.wait()
    ain_copy.wait()

    def add_u(j, carry):
        part = jnp.dot(
            hid[j], ain[pl.ds(pl.multiple_of(j * width, width), width), :], preferred_element_type=f32
        )
        u_acc[...] = jnp.where(j == 0, part, u_acc[...] + part)
        return carry

    u_acc[...] = jnp.zeros(u_acc.shape, f32)
    lax.fori_loop(0, tiles, add_u, 0)
    for pair in range(2):
        rows = slice(pair * 256, (pair + 1) * 256)
        u_buf[me, pair] = pack_rows(fold_lanes(u_acc[rows], own_row[rows]))

    def forward_z(distance):
        @pl.when(me >= distance)
        def _():
            p = jnp.maximum(me - distance, 0)
            arrived(expert, p)

            @pl.when(me < 3)
            def _():
                to_right(p).start()

            to_across(p).start()
            to_core(expert, 0, p).start()

        @pl.when(me + distance <= 3)
        def _():
            p = jnp.minimum(me + distance, 3)
            arrived(expert, p)

            @pl.when(me > 0)
            def _():
                to_left(p).start()

            to_across(p).start()
            to_core(expert, 0, p).start()

    def forward_x(distance):
        def one(p):
            arrived(across, p)
            to_core(across, 1, p).start()

        if distance == 0:
            one(me)
            return

        @pl.when(me >= distance)
        def _():
            one(jnp.maximum(me - distance, 0))

        @pl.when(me + distance <= 3)
        def _():
            one(jnp.minimum(me + distance, 3))

    def transpose_tiles(j, carry):
        hid_t[j] = hid[j].T
        return carry

    forward_z(1)
    forward_x(0)
    lax.fori_loop(0, tiles, transpose_tiles, 0)
    turned_copy = pltpu.make_async_copy(hid_t, turned_out, out_sem.at[0])
    turned_copy.start()
    forward_z(2)
    forward_x(1)

    def dispatch(pair):
        for i in range(2):
            p = pair * 2 + i
            arrived(core, p)
            arrived(diagonal, p)
            for q in range(4):
                disp[q, pair, i * LANES : (i + 1) * LANES, :] = jnp.dot(
                    place[p], tok[q, p], preferred_element_type=f32
                ).astype(bf16)

    def make_v(pair):
        rows = pl.ds(pl.multiple_of(pair * 256, 256), 256)
        values = dot_nt(disp[me, pair], aup[...])
        v_sum[rows] = fold_lanes(values, own_row[rows])
        v_buf[me, pair] = pack_rows(v_sum[rows])

    def send_v(pair, slot):
        copies = []
        for step in range(1, 4):
            copy = remote(
                v_buf.at[me, pair],
                v_buf.at[me, pair],
                v_send.at[slot, step - 1],
                v_recv.at[me, pair],
                dp=lax.rem(me + step, 4),
            )
            copy.start()
            copies.append(copy)
        return copies

    def base_tiles(pair, first, last):
        rows = pl.ds(pl.multiple_of(pair * 256, 256), 256)

        def tile(j, carry):
            total = dot_nt(disp[0, pair], down_v[j, :, 0:768])
            for q in range(1, 4):
                total = total + dot_nt(disp[q, pair], down_v[j, :, q * 768 : (q + 1) * 768])
            base[j, pair] = total
            product = hid[j, rows, :].astype(f32) * total
            for part in range(width // LANES):
                score_acc[rows] += product[:, part * LANES : (part + 1) * LANES]
            return carry

        lax.fori_loop(first, last, tile, 0)

    own_copy.wait()
    score_acc[...] = jnp.zeros(score_acc.shape, f32)
    dispatch(near)
    aup_copy.wait()
    make_v(near)
    for copy in down_copies:
        copy.wait()
    half = tiles // 2
    base_tiles(near, 0, half)
    forward_z(3)
    v_copies = send_v(near, 0)
    u_copies = []
    for step in range(1, 4):
        copy = remote(
            u_buf.at[me],
            u_buf.at[me],
            u_send.at[step - 1],
            u_recv.at[me],
            dp=lax.rem(me + step, 4),
        )
        copy.start()
        u_copies.append(copy)
    forward_x(2)
    base_tiles(near, half, tiles)

    forward_x(3)
    dispatch(far)
    make_v(far)
    v_copies += send_v(far, 1)
    feat_copy = pltpu.make_async_copy(disp.at[me], feat_out, out_sem.at[1])
    feat_copy.start()
    base_tiles(far, 0, tiles)

    for step in range(1, 4):
        p = lax.rem(me + step, 4)
        remote(u_buf.at[p], u_buf.at[p], u_send.at[0], u_recv.at[p], dp=p).wait_recv()
    for pair in range(2):
        rows = slice(pair * 256, (pair + 1) * 256)
        total = ((u_buf[0, pair] + u_buf[1, pair]) + u_buf[2, pair]) + u_buf[3, pair]
        total = unpack_rows(total)
        u_sum[rows] = total
        sc_ut[:, rows] = spread_rows(w_row[rows] * total, own_row[rows]).T.astype(bf16)
    sc_ut_copy = pltpu.make_async_copy(sc_ut, sc_ut_out, out_sem.at[2])
    sc_ut_copy.start()

    score_acc[...] += (adapter_scale / 4) * u_sum[...] * v_sum[...]
    for p in range(4):
        rows = slice(p * LANES, (p + 1) * LANES)
        score = jnp.sum(score_acc[rows], axis=1, keepdims=True)
        score_out[p] = jnp.sum(place[p].astype(f32) * score, axis=0, keepdims=True)
    score_copies = []
    for step in range(1, 16):
        p = lax.rem(me + step // 4, 4)
        copy = remote(
            score_out.at[p],
            score_in.at[me, expert],
            score_send.at[step - 1],
            score_recv.at[me, expert],
            dp=p,
            expert=lax.rem(expert + step % 4, 4),
        )
        copy.start()
        score_copies.append(copy)
    score_in[me, expert] = score_out[me]

    for step in range(1, 4):
        p = lax.rem(me + step, 4)
        for pair in range(2):
            remote(
                v_buf.at[p, pair],
                v_buf.at[p, pair],
                v_send.at[0, 0],
                v_recv.at[p, pair],
                dp=p,
            ).wait_recv()
    for pair in range(2):
        rows = slice(pair * 256, (pair + 1) * 256)
        total = ((v_buf[0, pair] + v_buf[1, pair]) + v_buf[2, pair]) + v_buf[3, pair]
        total = unpack_rows(total)
        sp_v[rows] = spread_rows(total, own_row[rows]).astype(bf16)
        sc_v[rows] = spread_rows(w_row[rows] * total, own_row[rows]).astype(bf16)

    sc_v_copy = pltpu.make_async_copy(sc_v, sc_v_out, out_sem.at[3])
    sc_v_copy.start()

    def out_hidden(j):
        return pltpu.make_async_copy(hg_v.at[j], hgrad_out.at[j], out_sem_hg.at[j])

    def finish(j, carry):
        extra = dot_nt(
            sp_v[...], ain[pl.ds(pl.multiple_of(j * width, width), width), :]
        )
        scale = w_row[...]
        scale = jnp.concatenate([scale] * (width // LANES), axis=1)
        hg_v[j] = (
            scale * (base[j].reshape(512, width) + adapter_scale * extra)
        ).astype(bf16)
        out_hidden(j).start()
        return carry

    lax.fori_loop(0, tiles, finish, 0)

    for step in range(1, 16):
        p = lax.rem(me + step // 4, 4)
        e = lax.rem(expert + step % 4, 4)
        block = score_in.at[p, e]
        remote(
            block, block, score_send.at[0], score_recv.at[p, e], dp=p, expert=e
        ).wait_recv()
    chosen = meta[me, 0:2, :]
    total = jnp.zeros((2, LANES), f32)
    for e in range(4):
        score = ((score_in[0, e] + score_in[1, e]) + score_in[2, e]) + score_in[3, e]
        total = total + jnp.where(chosen == float(e), score, 0.0)
    router_out[...] = total

    for copy in meta_copies + u_copies + v_copies + score_copies:
        copy.wait_send()
    for p in range(4):
        to_across(p).wait_send()
        to_core(expert, 0, p).wait_send()
        to_core(across, 1, p).wait_send()

        @pl.when((me > 0) & (me <= p))
        def _():
            to_left(p).wait_send()

        @pl.when((me < 3) & (me >= p))
        def _():
            to_right(p).wait_send()

    turned_copy.wait()
    feat_copy.wait()
    sc_ut_copy.wait()
    sc_v_copy.wait()
    for j in range(tiles):
        out_hidden(j).wait()


def products_kernel(hg, turned, scaled_v, scaled_ut, feat, router, hgrad, dgrad, ugrad, router_out):
    width = turned.shape[1]
    for part in range(turned.shape[0]):
        hgrad[0, :, part * width : (part + 1) * width] = hg[part]
        dgrad[0, part * width : (part + 1) * width, :] = adapter_scale * jnp.dot(
            turned[part], scaled_v[...], preferred_element_type=jnp.float32
        )
    ugrad[0] = adapter_scale * jnp.dot(
        scaled_ut[...], feat[...], preferred_element_type=jnp.float32
    )
    router_out[...] = router[...]


def kernel_body(
    output_gradient,
    hidden,
    down_matrix,
    adapter_down_matrix,
    adapter_up_matrix,
    routes,
    router_weight,
    tenant,
):
    width = 256
    tokens, features = output_gradient.shape
    _, slots, units = hidden.shape
    model = down_matrix.shape[2]
    spread = adapter_down_matrix.shape[2]
    tiles = units // width
    f32 = jnp.float32
    bf16 = jnp.bfloat16
    dma = pltpu.SemaphoreType.DMA
    vmem = pl.BlockSpec(memory_space=pltpu.VMEM)
    hbm = pl.BlockSpec(memory_space=pl.ANY)
    hg, turned, scaled_v, scaled_ut, feat, router = pl.pallas_call(
        functools.partial(kernel, tiles),
        out_shape=(
            jax.ShapeDtypeStruct((tiles, slots, width), bf16),
            jax.ShapeDtypeStruct((tiles, width, slots), bf16),
            jax.ShapeDtypeStruct((slots, spread), bf16),
            jax.ShapeDtypeStruct((spread, slots), bf16),
            jax.ShapeDtypeStruct((2, 256, features), bf16),
            jax.ShapeDtypeStruct((2, tokens), f32),
        ),
        in_specs=[hbm] * 5 + [vmem] * 3,
        out_specs=(hbm, hbm, hbm, hbm, hbm, vmem),
        scratch_shapes=[
            pltpu.VMEM((4, 4, tokens, features), bf16),
            pltpu.VMEM((4, 2, 256, features), bf16),
            pltpu.VMEM((tiles, width, model), bf16),
            pltpu.VMEM((tiles, slots, width), bf16),
            pltpu.VMEM((tiles, width, slots), bf16),
            pltpu.VMEM((units, spread), bf16),
            pltpu.VMEM((spread, features), bf16),
            pltpu.VMEM((tiles, 2, 256, width), f32),
            pltpu.VMEM((tiles, slots, width), bf16),
            pltpu.VMEM((slots, spread), f32),
            pltpu.VMEM((4, 8, LANES), f32),
            pltpu.VMEM((4, LANES, LANES), bf16),
            pltpu.VMEM((slots, LANES), f32),
            pltpu.VMEM((slots, LANES), f32),
            pltpu.VMEM((4, 2, 64, LANES), f32),
            pltpu.VMEM((4, 2, 64, LANES), f32),
            pltpu.VMEM((slots, LANES), f32),
            pltpu.VMEM((slots, LANES), f32),
            pltpu.VMEM((slots, spread), bf16),
            pltpu.VMEM((slots, spread), bf16),
            pltpu.VMEM((spread, slots), bf16),
            pltpu.VMEM((slots, LANES), f32),
            pltpu.VMEM((4, 1, LANES), f32),
            pltpu.VMEM((4, 4, 1, LANES), f32),
            dma((4, 4)),
            dma((2, 4)),
            dma((4,)),
            dma((2, 4)),
            dma((3,)),
            dma((4,)),
            dma((3,)),
            dma((4,)),
            dma((2, 3)),
            dma((4, 2)),
            dma((15,)),
            dma((4, 4)),
            dma((3,)),
            dma((tiles,)),
            dma((tiles,)),
            dma((4,)),
            dma((tiles,)),
        ],
        compiler_params=pltpu.CompilerParams(
            collective_id=0, has_side_effects=True, vmem_limit_bytes=58 * 1024 * 1024
        ),
    )(
        output_gradient,
        hidden,
        down_matrix,
        adapter_down_matrix,
        adapter_up_matrix,
        routes.T,
        router_weight.T,
        tenant[None, :],
    )
    group = 2
    steps = tiles // group
    whole = lambda j: (0, 0)
    hgrad, dgrad, ugrad, router = pl.pallas_call(
        products_kernel,
        grid=(steps,),
        out_shape=(
            jax.ShapeDtypeStruct(hidden.shape, bf16),
            jax.ShapeDtypeStruct(adapter_down_matrix.shape, f32),
            jax.ShapeDtypeStruct(adapter_up_matrix.shape, f32),
            jax.ShapeDtypeStruct((2, tokens), f32),
        ),
        in_specs=[
            pl.BlockSpec((group, slots, width), lambda j: (j, 0, 0)),
            pl.BlockSpec((group, width, slots), lambda j: (j, 0, 0)),
            pl.BlockSpec((slots, spread), whole),
            pl.BlockSpec((spread // steps, slots), lambda j: (j, 0)),
            pl.BlockSpec((slots, features), whole),
            pl.BlockSpec((2, tokens), whole),
        ],
        out_specs=(
            pl.BlockSpec((1, slots, group * width), lambda j: (0, 0, j)),
            pl.BlockSpec((1, group * width, spread), lambda j: (0, j, 0)),
            pl.BlockSpec((1, spread // steps, features), lambda j: (0, j, 0)),
            pl.BlockSpec((2, tokens), whole),
        ),
        compiler_params=pltpu.CompilerParams(vmem_limit_bytes=58 * 1024 * 1024),
    )(hg, turned, scaled_v, scaled_ut, feat.reshape(slots, features), router)
    return hgrad, dgrad, ugrad, router.T


def fitting_body(mesh, *arrays):
    gradient, hidden, down = arrays[0], arrays[1], arrays[2]
    fits = (
        mesh.shape["dp"] == 4
        and mesh.shape["expert"] == 4
        and gradient.shape == (128, 768)
        and hidden.shape[1] == 512
        and hidden.shape[2] == 2048
        and down.shape[2] == 3072
    )
    return (kernel_body if fits else body)(*arrays)


def solution(mesh):
    in_specs = (
        P(("groups", "dp"), "expert"),
        P("expert", "groups", "dp"),
        P("expert", "dp", None),
        P("expert", "dp", None),
        P("expert", None, "dp"),
        P(("groups", "dp"), None),
        P(("groups", "dp"), None),
        P(("groups", "dp")),
    )
    out_specs = (
        P("expert", "groups", "dp"),
        P(("groups", "expert"), "dp", None),
        P(("groups", "expert"), None, "dp"),
        P(("groups", "dp"), None),
    )
    return jax.shard_map(
        functools.partial(fitting_body, mesh),
        mesh=mesh,
        in_specs=in_specs,
        out_specs=out_specs,
        check_vma=False,
    )
```

```python
import functools

import jax
import jax.numpy as jnp
from jax import lax
from jax.experimental import pallas as pl
from jax.experimental.pallas import tpu as pltpu
from jax.sharding import PartitionSpec as P

ADAPTER_RANK = 32
TENANT_COUNT = 16


adapter_scale = 2.0


def slot_places(routes, experts, capacity):
    sources = routes.shape[0]
    flattened = routes.reshape(sources, -1)
    expert_hits = (
        flattened[:, :, None] == jnp.arange(experts, dtype=jnp.int32)[None, None, :]
    ).astype(jnp.int32)
    earlier = jnp.cumsum(expert_hits, axis=1) - expert_hits
    offset = jnp.sum(earlier * expert_hits, axis=2)
    target = flattened * capacity + offset
    return target[:, None, :] == jnp.arange(experts * capacity, dtype=jnp.int32)[None, :, None]


def tenant_mask(owner):
    return (owner[:, None] == jnp.arange(TENANT_COUNT, dtype=jnp.int32)[None, :]).astype(
        jnp.float32
    )


def select_rank_columns(matrix, owning_tenants):
    return jnp.sum(
        matrix.reshape(owning_tenants.shape[0], TENANT_COUNT, ADAPTER_RANK)
        * owning_tenants[:, :, None],
        axis=1,
    )


def expand_rank(values, owning_tenants):
    return (owning_tenants[:, :, None] * values[:, None, :]).reshape(
        owning_tenants.shape[0], TENANT_COUNT * ADAPTER_RANK
    )


def contract_matrices(left, right, left_dim, right_dim):
    return lax.dot_general(
        left, right, (((left_dim,), (right_dim,)), ((), ())), preferred_element_type=jnp.float32
    )


def rows_terms(
    dispatched,
    weight_slot,
    owner_slot,
    hidden_activation_rows,
    down_rows,
    adapter_input,
    adapter_output,
    shard_index,
):
    owning_tenants = tenant_mask(owner_slot)
    block_width = adapter_output.shape[1]
    feature_tile = lax.dynamic_slice_in_dim(dispatched, shard_index * block_width, block_width, 1)
    frozen_gradient = contract_matrices(dispatched, down_rows, 1, 1)
    inner_left_factor = select_rank_columns(
        jnp.dot(hidden_activation_rows, adapter_input, preferred_element_type=jnp.float32),
        owning_tenants,
    )
    inner_right_factor = select_rank_columns(
        contract_matrices(feature_tile, adapter_output, 1, 1), owning_tenants
    )
    partial_score = jnp.sum(hidden_activation_rows.astype(jnp.float32) * frozen_gradient, axis=1)
    return (
        frozen_gradient,
        inner_left_factor,
        inner_right_factor,
        partial_score,
        weight_slot.astype(jnp.float32),
        owner_slot,
        feature_tile,
    )


def body(
    output_gradient,
    hidden,
    down_matrix,
    adapter_down_matrix,
    adapter_up_matrix,
    routes,
    router_weight,
    tenant,
):
    experts = lax.axis_size("expert")
    expert_index = lax.axis_index("expert")
    shard_index = lax.axis_index("dp")
    token_count = output_gradient.shape[0]
    capacity = 4 * token_count // experts
    hidden_activation_rows = hidden[0]
    down_rows = down_matrix[0]
    adapter_input = adapter_down_matrix[0]
    adapter_output = adapter_up_matrix[0]
    own_table = slot_places(routes[None], experts, capacity)[0]
    token_match = (
        own_table.reshape(experts * capacity, token_count, 2).astype(jnp.bfloat16).sum(axis=2)
    )
    outgoing = jnp.dot(token_match, output_gradient, preferred_element_type=jnp.float32).astype(
        jnp.bfloat16
    )
    outgoing = outgoing.reshape(experts, capacity, -1)
    arrived = lax.all_to_all(outgoing, "expert", split_axis=0, concat_axis=2, tiled=True)[0]
    chosen = lax.dynamic_slice_in_dim(own_table, expert_index * capacity, capacity, 0)
    weight_slot = jnp.sum(
        jnp.where(chosen, router_weight.reshape(1, -1).astype(jnp.float32), 0.0), axis=1
    ).astype(jnp.bfloat16)
    owner_slot = jnp.sum(jnp.where(chosen, jnp.repeat(tenant, 2)[None, :], 0), axis=1)
    portion = lax.all_gather((arrived, weight_slot, owner_slot), "dp", axis=0, tiled=True)
    results = rows_terms(
        portion[0],
        portion[1],
        portion[2],
        hidden_activation_rows,
        down_rows,
        adapter_input,
        adapter_output,
        shard_index,
    )
    (
        frozen_gradient,
        inner_left_factor,
        inner_right_factor,
        partial_score,
        weight_float,
        owner_all,
        feature_tile,
    ) = results
    inner_left_factor, inner_right_factor = lax.psum((inner_left_factor, inner_right_factor), "dp")
    owned_score = lax.psum_scatter(partial_score, "dp", scatter_dimension=0, tiled=True)
    owned_left_factor = lax.dynamic_slice_in_dim(
        inner_left_factor, shard_index * capacity, capacity, 0
    )
    owned_right_factor = lax.dynamic_slice_in_dim(
        inner_right_factor, shard_index * capacity, capacity, 0
    )
    owned_score = owned_score + adapter_scale * jnp.sum(
        owned_left_factor * owned_right_factor, axis=1
    )
    returned = lax.all_gather(owned_score, "expert", axis=0, tiled=True)
    router_gradient = jnp.sum(jnp.where(own_table, returned[:, None], 0.0), axis=0).reshape(
        token_count, 2
    )
    owning_tenants = tenant_mask(owner_all)
    scale_factor = weight_float[:, None]
    spread_right_factor = expand_rank(inner_right_factor, owning_tenants)
    scaled_right_factor = (scale_factor * spread_right_factor).astype(jnp.bfloat16)
    scaled_left_factor = (scale_factor * expand_rank(inner_left_factor, owning_tenants)).astype(
        jnp.bfloat16
    )
    adapter_contribution = contract_matrices(
        spread_right_factor.astype(jnp.bfloat16), adapter_input, 1, 1
    )
    hidden_gradient = (
        scale_factor * (frozen_gradient + adapter_scale * adapter_contribution)
    ).astype(jnp.bfloat16)
    first_route_gradient = adapter_scale * contract_matrices(
        hidden_activation_rows, scaled_right_factor, 0, 0
    )
    second_route_gradient = adapter_scale * contract_matrices(
        scaled_left_factor, feature_tile, 0, 0
    )
    return (
        hidden_gradient[None],
        first_route_gradient[None],
        second_route_gradient[None],
        router_gradient,
    )


MESH = pl.DeviceIdType.MESH
LANES = 128
CHUNKS = 4


def dot_nt(left, right):
    return contract_matrices(left, right, 1, 1)


def fold_lanes(values, owners):
    lane_group = lax.broadcasted_iota(jnp.int32, owners.shape, 1) // ADAPTER_RANK
    total = jnp.zeros(owners.shape, jnp.float32)
    for part in range(TENANT_COUNT * ADAPTER_RANK // LANES):
        mine = owners == (lane_group + part * (LANES // ADAPTER_RANK)).astype(jnp.float32)
        total = total + jnp.where(mine, values[:, part * LANES : (part + 1) * LANES], 0.0)
    return repeat_groups(total)


def repeat_groups(values):
    values = values + pltpu.roll(values, 2 * ADAPTER_RANK, 1)
    return values + pltpu.roll(values, ADAPTER_RANK, 1)


def pack_rows(values):
    rows = values.shape[0] // 4
    lane_group = lax.broadcasted_iota(jnp.int32, (rows, LANES), 1) // ADAPTER_RANK
    total = values[:rows]
    for part in range(1, 4):
        total = jnp.where(lane_group == part, values[part * rows : (part + 1) * rows], total)
    return total


def unpack_rows(values):
    lane_group = lax.broadcasted_iota(jnp.int32, values.shape, 1) // ADAPTER_RANK
    return jnp.concatenate(
        [repeat_groups(jnp.where(lane_group == part, values, 0.0)) for part in range(4)], axis=0
    )


def spread_rows(values, owners):
    lane_group = lax.broadcasted_iota(jnp.int32, owners.shape, 1) // ADAPTER_RANK
    parts = []
    for part in range(TENANT_COUNT * ADAPTER_RANK // LANES):
        mine = owners == (lane_group + part * (LANES // ADAPTER_RANK)).astype(jnp.float32)
        parts.append(jnp.where(mine, values, 0.0))
    return jnp.concatenate(parts, axis=1)


def kernel(
    tiles,
    grad_ref,
    hidden_ref,
    down_ref,
    adown_ref,
    aup_ref,
    routes_ref,
    weight_ref,
    tenant_ref,
    hgrad_out,
    turned_out,
    sc_v_out,
    sc_ut_out,
    feat_out,
    router_out,
    tok,
    disp,
    down_v,
    hid,
    hid_t,
    ain,
    aup,
    base,
    hg_v,
    u_acc,
    meta,
    place,
    w_row,
    own_row,
    u_buf,
    v_buf,
    u_sum,
    v_sum,
    sp_v,
    sc_v,
    sc_ut,
    score_acc,
    score_out,
    score_in,
    tok_recv,
    send_z,
    send_x,
    send_c,
    meta_send,
    meta_recv,
    u_send,
    u_recv,
    v_send,
    v_recv,
    score_send,
    score_recv,
    load_sem,
    down_sem,
    hid_sem,
    out_sem,
    out_sem_hg,
):
    me = lax.axis_index("dp")
    expert = lax.axis_index("expert")
    across = lax.rem(expert + 2, 4)
    core = expert + 1 - 2 * lax.rem(expert, 2)
    diagonal = lax.rem(core + 2, 4)
    near = me // 2
    far = 1 - near
    width = hid.shape[2]
    f32 = jnp.float32
    bf16 = jnp.bfloat16

    own_copy = pltpu.make_async_copy(grad_ref, tok.at[expert, me], load_sem.at[0])
    ain_copy = pltpu.make_async_copy(adown_ref.at[0], ain, load_sem.at[1])
    aup_copy = pltpu.make_async_copy(aup_ref.at[0], aup, load_sem.at[2])
    hid_copies = [
        pltpu.make_async_copy(
            hidden_ref.at[0, :, pl.ds(j * width, width)], hid.at[j], hid_sem.at[j]
        )
        for j in range(tiles)
    ]
    down_copies = [
        pltpu.make_async_copy(
            down_ref.at[0, pl.ds(j * width, width), :], down_v.at[j], down_sem.at[j]
        )
        for j in range(tiles)
    ]
    own_copy.start()
    for copy in hid_copies:
        copy.start()
    ain_copy.start()
    aup_copy.start()
    for copy in down_copies:
        copy.start()
    meta[me, 0:2, :] = routes_ref[...].astype(f32)
    meta[me, 2:4, :] = weight_ref[...].astype(f32)
    meta[me, 4:5, :] = tenant_ref[...].astype(f32)
    meta[me, 5:8, :] = jnp.zeros((3, LANES), f32)

    barrier = pltpu.get_barrier_semaphore()
    for step in range(1, 16):
        pl.semaphore_signal(
            barrier,
            inc=1,
            device_id={
                "dp": lax.rem(me + step // 4, 4),
                "expert": lax.rem(expert + step % 4, 4),
            },
            device_id_type=MESH,
        )
    pl.semaphore_wait(barrier, 15)

    def remote(src, dst, send, recv, **target):
        return pltpu.make_async_remote_copy(
            src_ref=src,
            dst_ref=dst,
            send_sem=send,
            recv_sem=recv,
            device_id=target,
            device_id_type=MESH,
        )

    chunk_rows = tok.shape[2] // CHUNKS

    def chunk(ref, i):
        return ref.at[pl.ds(i * chunk_rows, chunk_rows)]

    def send(i, q, p, src, sent, **target):
        block = chunk(tok.at[q, p], i)
        return remote(
            block if src is None else chunk(src, i), block, sent, tok_recv.at[q, p, i], **target
        )

    def to_left(i, p, src=None):
        return send(i, expert, p, src, send_z.at[0, p, i], dp=jnp.maximum(me - 1, 0))

    def to_right(i, p, src=None):
        return send(i, expert, p, src, send_z.at[1, p, i], dp=jnp.minimum(me + 1, 3))

    def to_across(i, p, src=None):
        return send(i, expert, p, src, send_x.at[p, i], expert=across)

    def to_core(i, q, slot, p, src=None):
        return send(i, q, p, src, send_c.at[slot, p, i], expert=core)

    def arrived(i, q, p):
        send(i, q, p, None, send_c.at[0, p, i], expert=core).wait_recv()

    meta_copies = []
    for step in range(1, 4):
        copy = remote(
            meta.at[me],
            meta.at[me],
            meta_send.at[step - 1],
            meta_recv.at[me],
            dp=lax.rem(me + step, 4),
        )
        copy.start()
        meta_copies.append(copy)

    for i in range(CHUNKS):

        @pl.when(me > 0)
        def _():
            to_left(i, me, grad_ref).start()

        @pl.when(me < 3)
        def _():
            to_right(i, me, grad_ref).start()

        to_across(i, me, grad_ref).start()
    for i in range(CHUNKS):
        to_core(i, expert, 0, me, grad_ref).start()

    def forward_z(i, distance):
        @pl.when(me >= distance)
        def _():
            p = jnp.maximum(me - distance, 0)
            arrived(i, expert, p)

            @pl.when(me < 3)
            def _():
                to_right(i, p).start()

            to_across(i, p).start()
            to_core(i, expert, 0, p).start()

        @pl.when(me + distance <= 3)
        def _():
            p = jnp.minimum(me + distance, 3)
            arrived(i, expert, p)

            @pl.when(me > 0)
            def _():
                to_left(i, p).start()

            to_across(i, p).start()
            to_core(i, expert, 0, p).start()

    def forward_x(i, distance):
        def one(p):
            arrived(i, across, p)
            to_core(i, across, 1, p).start()

        if distance == 0:
            one(me)
            return

        @pl.when(me >= distance)
        def _():
            one(jnp.maximum(me - distance, 0))

        @pl.when(me + distance <= 3)
        def _():
            one(jnp.minimum(me + distance, 3))

    def forward(distance):
        for i in range(CHUNKS):
            if distance <= 3:
                forward_z(i, distance)
            forward_x(i, distance - 1)

    for copy in hid_copies:
        copy.wait()

    def transpose_tiles(j, carry):
        hid_t[j] = hid[j].T
        return carry

    lax.fori_loop(0, tiles, transpose_tiles, 0)
    turned_copy = pltpu.make_async_copy(hid_t, turned_out, out_sem.at[0])
    turned_copy.start()
    forward(1)
    for step in range(1, 4):
        p = lax.rem(me + step, 4)
        remote(
            meta.at[p], meta.at[p], meta_send.at[0], meta_recv.at[p], dp=p
        ).wait_recv()
    expert_f = expert.astype(f32)
    row_ids = lax.broadcasted_iota(jnp.int32, (LANES, LANES), 0)
    col_ids = lax.broadcasted_iota(jnp.int32, (LANES, LANES), 1)
    before = (row_ids < col_ids).astype(bf16)
    for p in range(4):
        info = meta[p]
        first = info[0:1] == expert_f
        second = info[1:2] == expert_f
        hit = jnp.where(first | second, 1.0, 0.0)
        offset = jnp.dot(
            jnp.broadcast_to(hit, (16, LANES)).astype(bf16), before, preferred_element_type=f32
        )[0:1]
        offset = jnp.where(hit > 0.0, offset, -1.0)
        table = offset == row_ids.astype(f32)
        place[p] = jnp.where(table, 1.0, 0.0).astype(bf16)
        chosen = jnp.where(first, info[2:3], info[3:4])
        rows = pl.ds(p * LANES, LANES)
        w_row[rows] = jnp.broadcast_to(
            jnp.sum(jnp.where(table, chosen, 0.0), axis=1, keepdims=True), (LANES, LANES)
        )
        own_row[rows] = jnp.broadcast_to(
            jnp.sum(jnp.where(table, info[4:5], 0.0), axis=1, keepdims=True), (LANES, LANES)
        )

    forward(2)

    ain_copy.wait()

    def add_u(j, carry):
        part = jnp.dot(
            hid[j], ain[pl.ds(pl.multiple_of(j * width, width), width), :], preferred_element_type=f32
        )
        u_acc[...] = jnp.where(j == 0, part, u_acc[...] + part)
        return carry

    u_acc[...] = jnp.zeros(u_acc.shape, f32)
    lax.fori_loop(0, tiles, add_u, 0)
    for pair in range(2):
        rows = slice(pair * 256, (pair + 1) * 256)
        u_buf[me, pair] = pack_rows(fold_lanes(u_acc[rows], own_row[rows]))


    def dispatch(pair):
        for i in range(2):
            p = pair * 2 + i
            for j in range(CHUNKS):
                arrived(j, core, p)
                arrived(j, diagonal, p)
            for q in range(4):
                disp[q, pair, i * LANES : (i + 1) * LANES, :] = jnp.dot(
                    place[p], tok[q, p], preferred_element_type=f32
                ).astype(bf16)

    def make_v(pair):
        rows = pl.ds(pl.multiple_of(pair * 256, 256), 256)
        values = dot_nt(disp[me, pair], aup[...])
        v_sum[rows] = fold_lanes(values, own_row[rows])
        v_buf[me, pair] = pack_rows(v_sum[rows])

    def send_v(pair, slot):
        copies = []
        for step in range(1, 4):
            copy = remote(
                v_buf.at[me, pair],
                v_buf.at[me, pair],
                v_send.at[slot, step - 1],
                v_recv.at[me, pair],
                dp=lax.rem(me + step, 4),
            )
            copy.start()
            copies.append(copy)
        return copies

    def base_tiles(pair, first, last):
        rows = pl.ds(pl.multiple_of(pair * 256, 256), 256)

        def tile(j, carry):
            total = dot_nt(disp[0, pair], down_v[j, :, 0:768])
            for q in range(1, 4):
                total = total + dot_nt(disp[q, pair], down_v[j, :, q * 768 : (q + 1) * 768])
            base[j, pair] = total
            product = hid[j, rows, :].astype(f32) * total
            for part in range(width // LANES):
                score_acc[rows] += product[:, part * LANES : (part + 1) * LANES]
            return carry

        lax.fori_loop(first, last, tile, 0)

    forward(3)
    u_copies = []
    for step in range(1, 4):
        copy = remote(
            u_buf.at[me],
            u_buf.at[me],
            u_send.at[step - 1],
            u_recv.at[me],
            dp=lax.rem(me + step, 4),
        )
        copy.start()
        u_copies.append(copy)
    own_copy.wait()
    score_acc[...] = jnp.zeros(score_acc.shape, f32)
    dispatch(near)
    aup_copy.wait()
    make_v(near)
    v_copies = send_v(near, 0)
    for copy in down_copies:
        copy.wait()
    base_tiles(near, 0, tiles)
    forward(4)
    dispatch(far)
    make_v(far)
    v_copies += send_v(far, 1)
    feat_copy = pltpu.make_async_copy(disp.at[me], feat_out, out_sem.at[1])
    feat_copy.start()
    base_tiles(far, 0, tiles)

    for step in range(1, 4):
        p = lax.rem(me + step, 4)
        remote(u_buf.at[p], u_buf.at[p], u_send.at[0], u_recv.at[p], dp=p).wait_recv()
    for pair in range(2):
        rows = slice(pair * 256, (pair + 1) * 256)
        total = ((u_buf[0, pair] + u_buf[1, pair]) + u_buf[2, pair]) + u_buf[3, pair]
        total = unpack_rows(total)
        u_sum[rows] = total
        sc_ut[:, rows] = spread_rows(w_row[rows] * total, own_row[rows]).T.astype(bf16)
    sc_ut_copy = pltpu.make_async_copy(sc_ut, sc_ut_out, out_sem.at[2])
    sc_ut_copy.start()

    score_acc[...] += (adapter_scale / 4) * u_sum[...] * v_sum[...]
    for p in range(4):
        rows = slice(p * LANES, (p + 1) * LANES)
        score = jnp.sum(score_acc[rows], axis=1, keepdims=True)
        score_out[p] = jnp.sum(place[p].astype(f32) * score, axis=0, keepdims=True)
    score_copies = []
    for step in range(1, 16):
        p = lax.rem(me + step // 4, 4)
        copy = remote(
            score_out.at[p],
            score_in.at[me, expert],
            score_send.at[step - 1],
            score_recv.at[me, expert],
            dp=p,
            expert=lax.rem(expert + step % 4, 4),
        )
        copy.start()
        score_copies.append(copy)
    score_in[me, expert] = score_out[me]

    for step in range(1, 4):
        p = lax.rem(me + step, 4)
        for pair in range(2):
            remote(
                v_buf.at[p, pair],
                v_buf.at[p, pair],
                v_send.at[0, 0],
                v_recv.at[p, pair],
                dp=p,
            ).wait_recv()
    for pair in range(2):
        rows = slice(pair * 256, (pair + 1) * 256)
        total = ((v_buf[0, pair] + v_buf[1, pair]) + v_buf[2, pair]) + v_buf[3, pair]
        total = unpack_rows(total)
        sp_v[rows] = spread_rows(total, own_row[rows]).astype(bf16)
        sc_v[rows] = spread_rows(w_row[rows] * total, own_row[rows]).astype(bf16)

    sc_v_copy = pltpu.make_async_copy(sc_v, sc_v_out, out_sem.at[3])
    sc_v_copy.start()

    def out_hidden(j):
        return pltpu.make_async_copy(hg_v.at[j], hgrad_out.at[j], out_sem_hg.at[j])

    def finish(j, carry):
        extra = dot_nt(
            sp_v[...], ain[pl.ds(pl.multiple_of(j * width, width), width), :]
        )
        scale = w_row[...]
        scale = jnp.concatenate([scale] * (width // LANES), axis=1)
        hg_v[j] = (
            scale * (base[j].reshape(512, width) + adapter_scale * extra)
        ).astype(bf16)
        out_hidden(j).start()
        return carry

    lax.fori_loop(0, tiles, finish, 0)

    for step in range(1, 16):
        p = lax.rem(me + step // 4, 4)
        e = lax.rem(expert + step % 4, 4)
        block = score_in.at[p, e]
        remote(
            block, block, score_send.at[0], score_recv.at[p, e], dp=p, expert=e
        ).wait_recv()
    chosen = meta[me, 0:2, :]
    total = jnp.zeros((2, LANES), f32)
    for e in range(4):
        score = ((score_in[0, e] + score_in[1, e]) + score_in[2, e]) + score_in[3, e]
        total = total + jnp.where(chosen == float(e), score, 0.0)
    router_out[...] = total

    for copy in meta_copies + u_copies + v_copies + score_copies:
        copy.wait_send()
    for p in range(4):
        for i in range(CHUNKS):
            to_across(i, p).wait_send()
            to_core(i, expert, 0, p).wait_send()
            to_core(i, across, 1, p).wait_send()

            @pl.when((me > 0) & (me <= p))
            def _():
                to_left(i, p).wait_send()

            @pl.when((me < 3) & (me >= p))
            def _():
                to_right(i, p).wait_send()

    turned_copy.wait()
    feat_copy.wait()
    sc_ut_copy.wait()
    sc_v_copy.wait()
    for j in range(tiles):
        out_hidden(j).wait()


def products_kernel(hg, turned, scaled_v, scaled_ut, feat, router, hgrad, dgrad, ugrad, router_out):
    width = turned.shape[1]
    for part in range(turned.shape[0]):
        hgrad[0, :, part * width : (part + 1) * width] = hg[part]
        dgrad[0, part * width : (part + 1) * width, :] = adapter_scale * jnp.dot(
            turned[part], scaled_v[...], preferred_element_type=jnp.float32
        )
    ugrad[0] = adapter_scale * jnp.dot(
        scaled_ut[...], feat[...], preferred_element_type=jnp.float32
    )
    router_out[...] = router[...]


def kernel_body(
    output_gradient,
    hidden,
    down_matrix,
    adapter_down_matrix,
    adapter_up_matrix,
    routes,
    router_weight,
    tenant,
):
    width = 256
    tokens, features = output_gradient.shape
    _, slots, units = hidden.shape
    model = down_matrix.shape[2]
    spread = adapter_down_matrix.shape[2]
    tiles = units // width
    f32 = jnp.float32
    bf16 = jnp.bfloat16
    dma = pltpu.SemaphoreType.DMA
    vmem = pl.BlockSpec(memory_space=pltpu.VMEM)
    hbm = pl.BlockSpec(memory_space=pl.ANY)
    hg, turned, scaled_v, scaled_ut, feat, router = pl.pallas_call(
        functools.partial(kernel, tiles),
        out_shape=(
            jax.ShapeDtypeStruct((tiles, slots, width), bf16),
            jax.ShapeDtypeStruct((tiles, width, slots), bf16),
            jax.ShapeDtypeStruct((slots, spread), bf16),
            jax.ShapeDtypeStruct((spread, slots), bf16),
            jax.ShapeDtypeStruct((2, 256, features), bf16),
            jax.ShapeDtypeStruct((2, tokens), f32),
        ),
        in_specs=[hbm] * 5 + [vmem] * 3,
        out_specs=(hbm, hbm, hbm, hbm, hbm, vmem),
        scratch_shapes=[
            pltpu.VMEM((4, 4, tokens, features), bf16),
            pltpu.VMEM((4, 2, 256, features), bf16),
            pltpu.VMEM((tiles, width, model), bf16),
            pltpu.VMEM((tiles, slots, width), bf16),
            pltpu.VMEM((tiles, width, slots), bf16),
            pltpu.VMEM((units, spread), bf16),
            pltpu.VMEM((spread, features), bf16),
            pltpu.VMEM((tiles, 2, 256, width), f32),
            pltpu.VMEM((tiles, slots, width), bf16),
            pltpu.VMEM((slots, spread), f32),
            pltpu.VMEM((4, 8, LANES), f32),
            pltpu.VMEM((4, LANES, LANES), bf16),
            pltpu.VMEM((slots, LANES), f32),
            pltpu.VMEM((slots, LANES), f32),
            pltpu.VMEM((4, 2, 64, LANES), f32),
            pltpu.VMEM((4, 2, 64, LANES), f32),
            pltpu.VMEM((slots, LANES), f32),
            pltpu.VMEM((slots, LANES), f32),
            pltpu.VMEM((slots, spread), bf16),
            pltpu.VMEM((slots, spread), bf16),
            pltpu.VMEM((spread, slots), bf16),
            pltpu.VMEM((slots, LANES), f32),
            pltpu.VMEM((4, 1, LANES), f32),
            pltpu.VMEM((4, 4, 1, LANES), f32),
            dma((4, 4, CHUNKS)),
            dma((2, 4, CHUNKS)),
            dma((4, CHUNKS)),
            dma((2, 4, CHUNKS)),
            dma((3,)),
            dma((4,)),
            dma((3,)),
            dma((4,)),
            dma((2, 3)),
            dma((4, 2)),
            dma((15,)),
            dma((4, 4)),
            dma((3,)),
            dma((tiles,)),
            dma((tiles,)),
            dma((4,)),
            dma((tiles,)),
        ],
        compiler_params=pltpu.CompilerParams(
            collective_id=0, has_side_effects=True, vmem_limit_bytes=58 * 1024 * 1024
        ),
    )(
        output_gradient,
        hidden,
        down_matrix,
        adapter_down_matrix,
        adapter_up_matrix,
        routes.T,
        router_weight.T,
        tenant[None, :],
    )
    group = 2
    steps = tiles // group
    whole = lambda j: (0, 0)
    hgrad, dgrad, ugrad, router = pl.pallas_call(
        products_kernel,
        grid=(steps,),
        out_shape=(
            jax.ShapeDtypeStruct(hidden.shape, bf16),
            jax.ShapeDtypeStruct(adapter_down_matrix.shape, f32),
            jax.ShapeDtypeStruct(adapter_up_matrix.shape, f32),
            jax.ShapeDtypeStruct((2, tokens), f32),
        ),
        in_specs=[
            pl.BlockSpec((group, slots, width), lambda j: (j, 0, 0)),
            pl.BlockSpec((group, width, slots), lambda j: (j, 0, 0)),
            pl.BlockSpec((slots, spread), whole),
            pl.BlockSpec((spread // steps, slots), lambda j: (j, 0)),
            pl.BlockSpec((slots, features), whole),
            pl.BlockSpec((2, tokens), whole),
        ],
        out_specs=(
            pl.BlockSpec((1, slots, group * width), lambda j: (0, 0, j)),
            pl.BlockSpec((1, group * width, spread), lambda j: (0, j, 0)),
            pl.BlockSpec((1, spread // steps, features), lambda j: (0, j, 0)),
            pl.BlockSpec((2, tokens), whole),
        ),
        compiler_params=pltpu.CompilerParams(vmem_limit_bytes=58 * 1024 * 1024),
    )(hg, turned, scaled_v, scaled_ut, feat.reshape(slots, features), router)
    return hgrad, dgrad, ugrad, router.T


def fitting_body(mesh, *arrays):
    gradient, hidden, down = arrays[0], arrays[1], arrays[2]
    fits = (
        mesh.shape["dp"] == 4
        and mesh.shape["expert"] == 4
        and gradient.shape == (128, 768)
        and hidden.shape[1] == 512
        and hidden.shape[2] == 2048
        and down.shape[2] == 3072
    )
    return (kernel_body if fits else body)(*arrays)


def solution(mesh):
    in_specs = (
        P(("groups", "dp"), "expert"),
        P("expert", "groups", "dp"),
        P("expert", "dp", None),
        P("expert", "dp", None),
        P("expert", None, "dp"),
        P(("groups", "dp"), None),
        P(("groups", "dp"), None),
        P(("groups", "dp")),
    )
    out_specs = (
        P("expert", "groups", "dp"),
        P(("groups", "expert"), "dp", None),
        P(("groups", "expert"), None, "dp"),
        P(("groups", "dp"), None),
    )
    return jax.shard_map(
        functools.partial(fitting_body, mesh),
        mesh=mesh,
        in_specs=in_specs,
        out_specs=out_specs,
        check_vma=False,
    )
```

```python
import functools

import jax
import jax.numpy as jnp
from jax import lax
from jax.experimental import pallas as pl
from jax.experimental.pallas import tpu as pltpu
from jax.sharding import PartitionSpec as P

ADAPTER_RANK = 32
TENANT_COUNT = 16


adapter_scale = 2.0


def slot_places(routes, experts, capacity):
    sources = routes.shape[0]
    flattened = routes.reshape(sources, -1)
    expert_hits = (
        flattened[:, :, None] == jnp.arange(experts, dtype=jnp.int32)[None, None, :]
    ).astype(jnp.int32)
    earlier = jnp.cumsum(expert_hits, axis=1) - expert_hits
    offset = jnp.sum(earlier * expert_hits, axis=2)
    target = flattened * capacity + offset
    return target[:, None, :] == jnp.arange(experts * capacity, dtype=jnp.int32)[None, :, None]


def tenant_mask(owner):
    return (owner[:, None] == jnp.arange(TENANT_COUNT, dtype=jnp.int32)[None, :]).astype(
        jnp.float32
    )


def select_rank_columns(matrix, owning_tenants):
    return jnp.sum(
        matrix.reshape(owning_tenants.shape[0], TENANT_COUNT, ADAPTER_RANK)
        * owning_tenants[:, :, None],
        axis=1,
    )


def expand_rank(values, owning_tenants):
    return (owning_tenants[:, :, None] * values[:, None, :]).reshape(
        owning_tenants.shape[0], TENANT_COUNT * ADAPTER_RANK
    )


def contract_matrices(left, right, left_dim, right_dim):
    return lax.dot_general(
        left, right, (((left_dim,), (right_dim,)), ((), ())), preferred_element_type=jnp.float32
    )


def rows_terms(
    dispatched,
    weight_slot,
    owner_slot,
    hidden_activation_rows,
    down_rows,
    adapter_input,
    adapter_output,
    shard_index,
):
    owning_tenants = tenant_mask(owner_slot)
    block_width = adapter_output.shape[1]
    feature_tile = lax.dynamic_slice_in_dim(dispatched, shard_index * block_width, block_width, 1)
    frozen_gradient = contract_matrices(dispatched, down_rows, 1, 1)
    inner_left_factor = select_rank_columns(
        jnp.dot(hidden_activation_rows, adapter_input, preferred_element_type=jnp.float32),
        owning_tenants,
    )
    inner_right_factor = select_rank_columns(
        contract_matrices(feature_tile, adapter_output, 1, 1), owning_tenants
    )
    partial_score = jnp.sum(hidden_activation_rows.astype(jnp.float32) * frozen_gradient, axis=1)
    return (
        frozen_gradient,
        inner_left_factor,
        inner_right_factor,
        partial_score,
        weight_slot.astype(jnp.float32),
        owner_slot,
        feature_tile,
    )


def body(
    output_gradient,
    hidden,
    down_matrix,
    adapter_down_matrix,
    adapter_up_matrix,
    routes,
    router_weight,
    tenant,
):
    experts = lax.axis_size("expert")
    expert_index = lax.axis_index("expert")
    shard_index = lax.axis_index("dp")
    token_count = output_gradient.shape[0]
    capacity = 4 * token_count // experts
    hidden_activation_rows = hidden[0]
    down_rows = down_matrix[0]
    adapter_input = adapter_down_matrix[0]
    adapter_output = adapter_up_matrix[0]
    own_table = slot_places(routes[None], experts, capacity)[0]
    token_match = (
        own_table.reshape(experts * capacity, token_count, 2).astype(jnp.bfloat16).sum(axis=2)
    )
    outgoing = jnp.dot(token_match, output_gradient, preferred_element_type=jnp.float32).astype(
        jnp.bfloat16
    )
    outgoing = outgoing.reshape(experts, capacity, -1)
    arrived = lax.all_to_all(outgoing, "expert", split_axis=0, concat_axis=2, tiled=True)[0]
    chosen = lax.dynamic_slice_in_dim(own_table, expert_index * capacity, capacity, 0)
    weight_slot = jnp.sum(
        jnp.where(chosen, router_weight.reshape(1, -1).astype(jnp.float32), 0.0), axis=1
    ).astype(jnp.bfloat16)
    owner_slot = jnp.sum(jnp.where(chosen, jnp.repeat(tenant, 2)[None, :], 0), axis=1)
    portion = lax.all_gather((arrived, weight_slot, owner_slot), "dp", axis=0, tiled=True)
    results = rows_terms(
        portion[0],
        portion[1],
        portion[2],
        hidden_activation_rows,
        down_rows,
        adapter_input,
        adapter_output,
        shard_index,
    )
    (
        frozen_gradient,
        inner_left_factor,
        inner_right_factor,
        partial_score,
        weight_float,
        owner_all,
        feature_tile,
    ) = results
    inner_left_factor, inner_right_factor = lax.psum((inner_left_factor, inner_right_factor), "dp")
    owned_score = lax.psum_scatter(partial_score, "dp", scatter_dimension=0, tiled=True)
    owned_left_factor = lax.dynamic_slice_in_dim(
        inner_left_factor, shard_index * capacity, capacity, 0
    )
    owned_right_factor = lax.dynamic_slice_in_dim(
        inner_right_factor, shard_index * capacity, capacity, 0
    )
    owned_score = owned_score + adapter_scale * jnp.sum(
        owned_left_factor * owned_right_factor, axis=1
    )
    returned = lax.all_gather(owned_score, "expert", axis=0, tiled=True)
    router_gradient = jnp.sum(jnp.where(own_table, returned[:, None], 0.0), axis=0).reshape(
        token_count, 2
    )
    owning_tenants = tenant_mask(owner_all)
    scale_factor = weight_float[:, None]
    spread_right_factor = expand_rank(inner_right_factor, owning_tenants)
    scaled_right_factor = (scale_factor * spread_right_factor).astype(jnp.bfloat16)
    scaled_left_factor = (scale_factor * expand_rank(inner_left_factor, owning_tenants)).astype(
        jnp.bfloat16
    )
    adapter_contribution = contract_matrices(
        spread_right_factor.astype(jnp.bfloat16), adapter_input, 1, 1
    )
    hidden_gradient = (
        scale_factor * (frozen_gradient + adapter_scale * adapter_contribution)
    ).astype(jnp.bfloat16)
    first_route_gradient = adapter_scale * contract_matrices(
        hidden_activation_rows, scaled_right_factor, 0, 0
    )
    second_route_gradient = adapter_scale * contract_matrices(
        scaled_left_factor, feature_tile, 0, 0
    )
    return (
        hidden_gradient[None],
        first_route_gradient[None],
        second_route_gradient[None],
        router_gradient,
    )


MESH = pl.DeviceIdType.MESH
LANES = 128
CHUNKS = 4


def dot_nt(left, right):
    return contract_matrices(left, right, 1, 1)


def fold_lanes(values, owners):
    lane_group = lax.broadcasted_iota(jnp.int32, owners.shape, 1) // ADAPTER_RANK
    total = jnp.zeros(owners.shape, jnp.float32)
    for part in range(TENANT_COUNT * ADAPTER_RANK // LANES):
        mine = owners == (lane_group + part * (LANES // ADAPTER_RANK)).astype(jnp.float32)
        total = total + jnp.where(mine, values[:, part * LANES : (part + 1) * LANES], 0.0)
    return repeat_groups(total)


def repeat_groups(values):
    values = values + pltpu.roll(values, 2 * ADAPTER_RANK, 1)
    return values + pltpu.roll(values, ADAPTER_RANK, 1)


def pack_rows(values):
    rows = values.shape[0] // 4
    lane_group = lax.broadcasted_iota(jnp.int32, (rows, LANES), 1) // ADAPTER_RANK
    total = values[:rows]
    for part in range(1, 4):
        total = jnp.where(lane_group == part, values[part * rows : (part + 1) * rows], total)
    return total


def unpack_rows(values):
    lane_group = lax.broadcasted_iota(jnp.int32, values.shape, 1) // ADAPTER_RANK
    return jnp.concatenate(
        [repeat_groups(jnp.where(lane_group == part, values, 0.0)) for part in range(4)], axis=0
    )


def spread_rows(values, owners):
    lane_group = lax.broadcasted_iota(jnp.int32, owners.shape, 1) // ADAPTER_RANK
    parts = []
    for part in range(TENANT_COUNT * ADAPTER_RANK // LANES):
        mine = owners == (lane_group + part * (LANES // ADAPTER_RANK)).astype(jnp.float32)
        parts.append(jnp.where(mine, values, 0.0))
    return jnp.concatenate(parts, axis=1)


def kernel(
    tiles,
    grad_ref,
    hidden_ref,
    down_ref,
    adown_ref,
    aup_ref,
    routes_ref,
    weight_ref,
    tenant_ref,
    hgrad_out,
    turned_out,
    sc_v_out,
    sc_ut_out,
    feat_out,
    router_out,
    tok,
    disp,
    down_v,
    hid,
    hid_t,
    ain,
    aup,
    base,
    hg_v,
    u_acc,
    meta,
    place,
    w_row,
    own_row,
    u_buf,
    v_buf,
    u_sum,
    v_sum,
    sp_v,
    sc_v,
    sc_ut,
    score_acc,
    score_out,
    score_in,
    tok_recv,
    send_z,
    send_x,
    send_c,
    meta_send,
    meta_recv,
    u_send,
    u_recv,
    v_send,
    v_recv,
    score_send,
    score_recv,
    load_sem,
    down_sem,
    hid_sem,
    out_sem,
    out_sem_hg,
):
    me = lax.axis_index("dp")
    expert = lax.axis_index("expert")
    across = lax.rem(expert + 2, 4)
    core = expert + 1 - 2 * lax.rem(expert, 2)
    diagonal = lax.rem(core + 2, 4)
    near = me // 2
    far = 1 - near
    width = hid.shape[2]
    f32 = jnp.float32
    bf16 = jnp.bfloat16

    own_copy = pltpu.make_async_copy(grad_ref, tok.at[expert, me], load_sem.at[0])
    ain_copy = pltpu.make_async_copy(adown_ref.at[0], ain, load_sem.at[1])
    aup_copy = pltpu.make_async_copy(aup_ref.at[0], aup, load_sem.at[2])
    hid_copies = [
        pltpu.make_async_copy(
            hidden_ref.at[0, :, pl.ds(j * width, width)], hid.at[j], hid_sem.at[j]
        )
        for j in range(tiles)
    ]
    down_copies = [
        pltpu.make_async_copy(
            down_ref.at[0, pl.ds(j * width, width), :], down_v.at[j], down_sem.at[j]
        )
        for j in range(tiles)
    ]
    own_copy.start()
    for copy in hid_copies:
        copy.start()
    ain_copy.start()
    aup_copy.start()
    for copy in down_copies:
        copy.start()
    meta[me, 0:2, :] = routes_ref[...].astype(f32)
    meta[me, 2:4, :] = weight_ref[...].astype(f32)
    meta[me, 4:5, :] = tenant_ref[...].astype(f32)
    meta[me, 5:8, :] = jnp.zeros((3, LANES), f32)

    barrier = pltpu.get_barrier_semaphore()
    for step in range(1, 16):
        pl.semaphore_signal(
            barrier,
            inc=1,
            device_id={
                "dp": lax.rem(me + step // 4, 4),
                "expert": lax.rem(expert + step % 4, 4),
            },
            device_id_type=MESH,
        )
    pl.semaphore_wait(barrier, 15)

    def remote(src, dst, send, recv, **target):
        return pltpu.make_async_remote_copy(
            src_ref=src,
            dst_ref=dst,
            send_sem=send,
            recv_sem=recv,
            device_id=target,
            device_id_type=MESH,
        )

    chunk_rows = tok.shape[2] // CHUNKS

    def chunk(ref, i):
        return ref.at[pl.ds(i * chunk_rows, chunk_rows)]

    def send(i, q, p, src, sent, **target):
        block = chunk(tok.at[q, p], i)
        return remote(
            block if src is None else chunk(src, i), block, sent, tok_recv.at[q, p, i], **target
        )

    def to_left(i, p, src=None):
        return send(i, expert, p, src, send_z.at[0, p, i], dp=jnp.maximum(me - 1, 0))

    def to_right(i, p, src=None):
        return send(i, expert, p, src, send_z.at[1, p, i], dp=jnp.minimum(me + 1, 3))

    def to_across(i, p, src=None):
        return send(i, expert, p, src, send_x.at[p, i], expert=across)

    def to_core(i, q, slot, p, src=None):
        return send(i, q, p, src, send_c.at[slot, p, i], expert=core)

    def arrived(i, q, p):
        send(i, q, p, None, send_c.at[0, p, i], expert=core).wait_recv()

    meta_copies = []
    for step in range(1, 4):
        copy = remote(
            meta.at[me],
            meta.at[me],
            meta_send.at[step - 1],
            meta_recv.at[me],
            dp=lax.rem(me + step, 4),
        )
        copy.start()
        meta_copies.append(copy)

    for i in range(CHUNKS):

        @pl.when(me > 0)
        def _():
            to_left(i, me, grad_ref).start()

        @pl.when(me < 3)
        def _():
            to_right(i, me, grad_ref).start()

        to_across(i, me, grad_ref).start()
    for i in range(CHUNKS):
        to_core(i, expert, 0, me, grad_ref).start()

    def forward_z(i, distance):
        @pl.when(me >= distance)
        def _():
            p = jnp.maximum(me - distance, 0)
            arrived(i, expert, p)

            @pl.when(me < 3)
            def _():
                to_right(i, p).start()

            to_across(i, p).start()
            to_core(i, expert, 0, p).start()

        @pl.when(me + distance <= 3)
        def _():
            p = jnp.minimum(me + distance, 3)
            arrived(i, expert, p)

            @pl.when(me > 0)
            def _():
                to_left(i, p).start()

            to_across(i, p).start()
            to_core(i, expert, 0, p).start()

    def forward_x(i, distance):
        def one(p):
            arrived(i, across, p)
            to_core(i, across, 1, p).start()

        if distance == 0:
            one(me)
            return

        @pl.when(me >= distance)
        def _():
            one(jnp.maximum(me - distance, 0))

        @pl.when(me + distance <= 3)
        def _():
            one(jnp.minimum(me + distance, 3))

    def forward(distance):
        for i in range(CHUNKS):
            if distance <= 3:
                forward_z(i, distance)
            forward_x(i, distance - 1)

    for copy in hid_copies:
        copy.wait()

    def transpose_tiles(j, carry):
        hid_t[j] = hid[j].T
        return carry

    lax.fori_loop(0, tiles, transpose_tiles, 0)
    turned_copy = pltpu.make_async_copy(hid_t, turned_out, out_sem.at[0])
    turned_copy.start()
    forward(1)
    for step in range(1, 4):
        p = lax.rem(me + step, 4)
        remote(
            meta.at[p], meta.at[p], meta_send.at[0], meta_recv.at[p], dp=p
        ).wait_recv()
    expert_f = expert.astype(f32)
    row_ids = lax.broadcasted_iota(jnp.int32, (LANES, LANES), 0)
    col_ids = lax.broadcasted_iota(jnp.int32, (LANES, LANES), 1)
    before = (row_ids < col_ids).astype(bf16)
    for p in range(4):
        info = meta[p]
        first = info[0:1] == expert_f
        second = info[1:2] == expert_f
        hit = jnp.where(first | second, 1.0, 0.0)
        offset = jnp.dot(
            jnp.broadcast_to(hit, (16, LANES)).astype(bf16), before, preferred_element_type=f32
        )[0:1]
        offset = jnp.where(hit > 0.0, offset, -1.0)
        table = offset == row_ids.astype(f32)
        place[p] = jnp.where(table, 1.0, 0.0).astype(bf16)
        chosen = jnp.where(first, info[2:3], info[3:4])
        rows = pl.ds(p * LANES, LANES)
        w_row[rows] = jnp.broadcast_to(
            jnp.sum(jnp.where(table, chosen, 0.0), axis=1, keepdims=True), (LANES, LANES)
        )
        own_row[rows] = jnp.broadcast_to(
            jnp.sum(jnp.where(table, info[4:5], 0.0), axis=1, keepdims=True), (LANES, LANES)
        )

    forward(2)

    ain_copy.wait()

    def add_u(j, carry):
        part = jnp.dot(
            hid[j], ain[pl.ds(pl.multiple_of(j * width, width), width), :], preferred_element_type=f32
        )
        u_acc[...] = jnp.where(j == 0, part, u_acc[...] + part)
        return carry

    u_acc[...] = jnp.zeros(u_acc.shape, f32)
    lax.fori_loop(0, tiles, add_u, 0)
    for pair in range(2):
        rows = slice(pair * 256, (pair + 1) * 256)
        u_buf[me, pair] = pack_rows(fold_lanes(u_acc[rows], own_row[rows]))


    def dispatch(pair):
        for i in range(2):
            p = pair * 2 + i
            for j in range(CHUNKS):
                arrived(j, core, p)
                arrived(j, diagonal, p)
            for q in range(4):
                disp[q, pair, i * LANES : (i + 1) * LANES, :] = jnp.dot(
                    place[p], tok[q, p], preferred_element_type=f32
                ).astype(bf16)

    def make_v(pair):
        rows = pl.ds(pl.multiple_of(pair * 256, 256), 256)
        values = dot_nt(disp[me, pair], aup[...])
        v_sum[rows] = fold_lanes(values, own_row[rows])
        v_buf[me, pair] = pack_rows(v_sum[rows])

    def send_v(pair, slot):
        copies = []
        for step in range(1, 4):
            copy = remote(
                v_buf.at[me, pair],
                v_buf.at[me, pair],
                v_send.at[slot, step - 1],
                v_recv.at[me, pair],
                dp=lax.rem(me + step, 4),
            )
            copy.start()
            copies.append(copy)
        return copies

    def base_tiles(pair, first, last):
        rows = pl.ds(pl.multiple_of(pair * 256, 256), 256)

        def tile(j, carry):
            total = dot_nt(disp[0, pair], down_v[j, :, 0:768])
            for q in range(1, 4):
                total = total + dot_nt(disp[q, pair], down_v[j, :, q * 768 : (q + 1) * 768])
            base[j, pair] = total
            product = hid[j, rows, :].astype(f32) * total
            for part in range(width // LANES):
                score_acc[rows] += product[:, part * LANES : (part + 1) * LANES]
            return carry

        lax.fori_loop(first, last, tile, 0)

    forward(3)
    u_copies = []
    for step in range(1, 4):
        copy = remote(
            u_buf.at[me],
            u_buf.at[me],
            u_send.at[step - 1],
            u_recv.at[me],
            dp=lax.rem(me + step, 4),
        )
        copy.start()
        u_copies.append(copy)
    own_copy.wait()
    score_acc[...] = jnp.zeros(score_acc.shape, f32)
    dispatch(near)
    aup_copy.wait()
    make_v(near)
    v_copies = send_v(near, 0)
    for copy in down_copies:
        copy.wait()
    base_tiles(near, 0, tiles)
    for step in range(1, 4):
        p = lax.rem(me + step, 4)
        remote(u_buf.at[p], u_buf.at[p], u_send.at[0], u_recv.at[p], dp=p).wait_recv()
    for pair in range(2):
        rows = slice(pair * 256, (pair + 1) * 256)
        total = ((u_buf[0, pair] + u_buf[1, pair]) + u_buf[2, pair]) + u_buf[3, pair]
        total = unpack_rows(total)
        u_sum[rows] = total
        sc_ut[:, rows] = spread_rows(w_row[rows] * total, own_row[rows]).T.astype(bf16)
    sc_ut_copy = pltpu.make_async_copy(sc_ut, sc_ut_out, out_sem.at[2])
    sc_ut_copy.start()

    forward(4)
    dispatch(far)
    make_v(far)
    v_copies += send_v(far, 1)
    feat_copy = pltpu.make_async_copy(disp.at[me], feat_out, out_sem.at[1])
    feat_copy.start()
    base_tiles(far, 0, tiles)

    score_acc[...] += (adapter_scale / 4) * u_sum[...] * v_sum[...]
    for p in range(4):
        rows = slice(p * LANES, (p + 1) * LANES)
        score = jnp.sum(score_acc[rows], axis=1, keepdims=True)
        score_out[p] = jnp.sum(place[p].astype(f32) * score, axis=0, keepdims=True)
    score_copies = []
    for step in range(1, 16):
        p = lax.rem(me + step // 4, 4)
        copy = remote(
            score_out.at[p],
            score_in.at[me, expert],
            score_send.at[step - 1],
            score_recv.at[me, expert],
            dp=p,
            expert=lax.rem(expert + step % 4, 4),
        )
        copy.start()
        score_copies.append(copy)
    score_in[me, expert] = score_out[me]

    for step in range(1, 4):
        p = lax.rem(me + step, 4)
        for pair in range(2):
            remote(
                v_buf.at[p, pair],
                v_buf.at[p, pair],
                v_send.at[0, 0],
                v_recv.at[p, pair],
                dp=p,
            ).wait_recv()
    for pair in range(2):
        rows = slice(pair * 256, (pair + 1) * 256)
        total = ((v_buf[0, pair] + v_buf[1, pair]) + v_buf[2, pair]) + v_buf[3, pair]
        total = unpack_rows(total)
        sp_v[rows] = spread_rows(total, own_row[rows]).astype(bf16)
        sc_v[rows] = spread_rows(w_row[rows] * total, own_row[rows]).astype(bf16)

    sc_v_copy = pltpu.make_async_copy(sc_v, sc_v_out, out_sem.at[3])
    sc_v_copy.start()

    def out_hidden(j):
        return pltpu.make_async_copy(hg_v.at[j], hgrad_out.at[j], out_sem_hg.at[j])

    def finish(j, carry):
        extra = dot_nt(
            sp_v[...], ain[pl.ds(pl.multiple_of(j * width, width), width), :]
        )
        scale = w_row[...]
        scale = jnp.concatenate([scale] * (width // LANES), axis=1)
        hg_v[j] = (
            scale * (base[j].reshape(512, width) + adapter_scale * extra)
        ).astype(bf16)
        out_hidden(j).start()
        return carry

    lax.fori_loop(0, tiles, finish, 0)

    for step in range(1, 16):
        p = lax.rem(me + step // 4, 4)
        e = lax.rem(expert + step % 4, 4)
        block = score_in.at[p, e]
        remote(
            block, block, score_send.at[0], score_recv.at[p, e], dp=p, expert=e
        ).wait_recv()
    chosen = meta[me, 0:2, :]
    total = jnp.zeros((2, LANES), f32)
    for e in range(4):
        score = ((score_in[0, e] + score_in[1, e]) + score_in[2, e]) + score_in[3, e]
        total = total + jnp.where(chosen == float(e), score, 0.0)
    router_out[...] = total

    for copy in meta_copies + u_copies + v_copies + score_copies:
        copy.wait_send()
    for p in range(4):
        for i in range(CHUNKS):
            to_across(i, p).wait_send()
            to_core(i, expert, 0, p).wait_send()
            to_core(i, across, 1, p).wait_send()

            @pl.when((me > 0) & (me <= p))
            def _():
                to_left(i, p).wait_send()

            @pl.when((me < 3) & (me >= p))
            def _():
                to_right(i, p).wait_send()

    turned_copy.wait()
    feat_copy.wait()
    sc_ut_copy.wait()
    sc_v_copy.wait()
    for j in range(tiles):
        out_hidden(j).wait()


def products_kernel(hg, turned, scaled_v, scaled_ut, feat, router, hgrad, dgrad, ugrad, router_out):
    width = turned.shape[1]
    for part in range(turned.shape[0]):
        hgrad[0, :, part * width : (part + 1) * width] = hg[part]
        dgrad[0, part * width : (part + 1) * width, :] = adapter_scale * jnp.dot(
            turned[part], scaled_v[...], preferred_element_type=jnp.float32
        )
    ugrad[0] = adapter_scale * jnp.dot(
        scaled_ut[...], feat[...], preferred_element_type=jnp.float32
    )
    router_out[...] = router[...]


def kernel_body(
    output_gradient,
    hidden,
    down_matrix,
    adapter_down_matrix,
    adapter_up_matrix,
    routes,
    router_weight,
    tenant,
):
    width = 256
    tokens, features = output_gradient.shape
    _, slots, units = hidden.shape
    model = down_matrix.shape[2]
    spread = adapter_down_matrix.shape[2]
    tiles = units // width
    f32 = jnp.float32
    bf16 = jnp.bfloat16
    dma = pltpu.SemaphoreType.DMA
    vmem = pl.BlockSpec(memory_space=pltpu.VMEM)
    hbm = pl.BlockSpec(memory_space=pl.ANY)
    hg, turned, scaled_v, scaled_ut, feat, router = pl.pallas_call(
        functools.partial(kernel, tiles),
        out_shape=(
            jax.ShapeDtypeStruct((tiles, slots, width), bf16),
            jax.ShapeDtypeStruct((tiles, width, slots), bf16),
            jax.ShapeDtypeStruct((slots, spread), bf16),
            jax.ShapeDtypeStruct((spread, slots), bf16),
            jax.ShapeDtypeStruct((2, 256, features), bf16),
            jax.ShapeDtypeStruct((2, tokens), f32),
        ),
        in_specs=[hbm] * 5 + [vmem] * 3,
        out_specs=(hbm, hbm, hbm, hbm, hbm, vmem),
        scratch_shapes=[
            pltpu.VMEM((4, 4, tokens, features), bf16),
            pltpu.VMEM((4, 2, 256, features), bf16),
            pltpu.VMEM((tiles, width, model), bf16),
            pltpu.VMEM((tiles, slots, width), bf16),
            pltpu.VMEM((tiles, width, slots), bf16),
            pltpu.VMEM((units, spread), bf16),
            pltpu.VMEM((spread, features), bf16),
            pltpu.VMEM((tiles, 2, 256, width), f32),
            pltpu.VMEM((tiles, slots, width), bf16),
            pltpu.VMEM((slots, spread), f32),
            pltpu.VMEM((4, 8, LANES), f32),
            pltpu.VMEM((4, LANES, LANES), bf16),
            pltpu.VMEM((slots, LANES), f32),
            pltpu.VMEM((slots, LANES), f32),
            pltpu.VMEM((4, 2, 64, LANES), f32),
            pltpu.VMEM((4, 2, 64, LANES), f32),
            pltpu.VMEM((slots, LANES), f32),
            pltpu.VMEM((slots, LANES), f32),
            pltpu.VMEM((slots, spread), bf16),
            pltpu.VMEM((slots, spread), bf16),
            pltpu.VMEM((spread, slots), bf16),
            pltpu.VMEM((slots, LANES), f32),
            pltpu.VMEM((4, 1, LANES), f32),
            pltpu.VMEM((4, 4, 1, LANES), f32),
            dma((4, 4, CHUNKS)),
            dma((2, 4, CHUNKS)),
            dma((4, CHUNKS)),
            dma((2, 4, CHUNKS)),
            dma((3,)),
            dma((4,)),
            dma((3,)),
            dma((4,)),
            dma((2, 3)),
            dma((4, 2)),
            dma((15,)),
            dma((4, 4)),
            dma((3,)),
            dma((tiles,)),
            dma((tiles,)),
            dma((4,)),
            dma((tiles,)),
        ],
        compiler_params=pltpu.CompilerParams(
            collective_id=0, has_side_effects=True, vmem_limit_bytes=58 * 1024 * 1024
        ),
    )(
        output_gradient,
        hidden,
        down_matrix,
        adapter_down_matrix,
        adapter_up_matrix,
        routes.T,
        router_weight.T,
        tenant[None, :],
    )
    group = 1
    steps = tiles // group
    whole = lambda j: (0, 0)
    hgrad, dgrad, ugrad, router = pl.pallas_call(
        products_kernel,
        grid=(steps,),
        out_shape=(
            jax.ShapeDtypeStruct(hidden.shape, bf16),
            jax.ShapeDtypeStruct(adapter_down_matrix.shape, f32),
            jax.ShapeDtypeStruct(adapter_up_matrix.shape, f32),
            jax.ShapeDtypeStruct((2, tokens), f32),
        ),
        in_specs=[
            pl.BlockSpec((group, slots, width), lambda j: (j, 0, 0)),
            pl.BlockSpec((group, width, slots), lambda j: (j, 0, 0)),
            pl.BlockSpec((slots, spread), whole),
            pl.BlockSpec((spread // steps, slots), lambda j: (j, 0)),
            pl.BlockSpec((slots, features), whole),
            pl.BlockSpec((2, tokens), whole),
        ],
        out_specs=(
            pl.BlockSpec((1, slots, group * width), lambda j: (0, 0, j)),
            pl.BlockSpec((1, group * width, spread), lambda j: (0, j, 0)),
            pl.BlockSpec((1, spread // steps, features), lambda j: (0, j, 0)),
            pl.BlockSpec((2, tokens), whole),
        ),
        compiler_params=pltpu.CompilerParams(vmem_limit_bytes=58 * 1024 * 1024),
    )(hg, turned, scaled_v, scaled_ut, feat.reshape(slots, features), router)
    return hgrad, dgrad, ugrad, router.T


def fitting_body(mesh, *arrays):
    gradient, hidden, down = arrays[0], arrays[1], arrays[2]
    fits = (
        mesh.shape["dp"] == 4
        and mesh.shape["expert"] == 4
        and gradient.shape == (128, 768)
        and hidden.shape[1] == 512
        and hidden.shape[2] == 2048
        and down.shape[2] == 3072
    )
    return (kernel_body if fits else body)(*arrays)


def solution(mesh):
    in_specs = (
        P(("groups", "dp"), "expert"),
        P("expert", "groups", "dp"),
        P("expert", "dp", None),
        P("expert", "dp", None),
        P("expert", None, "dp"),
        P(("groups", "dp"), None),
        P(("groups", "dp"), None),
        P(("groups", "dp")),
    )
    out_specs = (
        P("expert", "groups", "dp"),
        P(("groups", "expert"), "dp", None),
        P(("groups", "expert"), None, "dp"),
        P(("groups", "dp"), None),
    )
    return jax.shard_map(
        functools.partial(fitting_body, mesh),
        mesh=mesh,
        in_specs=in_specs,
        out_specs=out_specs,
        check_vma=False,
    )
```
